128 devices in a mesh: row: 8 (over x, y_lo), col: 4 (over z), comp: 4 (over y_hi, core).
Axes of the slice: x: 4, y: 4 (y_hi: 2, y_lo: 2; y = y_hi * 2 + y_lo), z: 4, core: 2. Of those that a mesh axis runs over, the one named last changes fastest.
Arguments:
- features: bfloat16 [256, 1024, 512], P('row', ('col', 'comp')), may hold values from -6 to 6
- conv_weight: bfloat16 [3, 3, 512, 256], replicated, may hold values from -0.09375 to 0.09375
- conv_bias: float32 [256], replicated, may hold values from -3 to 3
- means: float32 [1024, 256], P('comp'), may hold values from -0.6 to 0.6
- precisions: float32 [1024, 256], P('comp'), may hold values from 0.7 to 1.3
- mix_logits: float32 [1024], replicated, may hold values from -4 to 4
- tissue_counts: int32 [8, 16], P('row', ('col', 'comp')), may hold values from 1 to 2048, as said below
Outputs:
- mean_fisher: float32 [1024, 256], P('comp')
- var_fisher: float32 [1024, 256], P('comp')
The draws below stay inside these ranges and needn't reach their ends.
Inputs may be any that keep to these rules, and one draw needn't show every extreme that they name: `tissue_counts`: a tile of tile row r holds at most 2048 * (r + 1) // 8 tissue patches; some tile is full.
All inputs are finite; a program needn't handle non-finite values.
Results may differ from the reference program's by a relative error of at most 0.0065.
The reference program's roundings to bfloat16 on the way (of `encoded`, `design`, `panel` and `gamma`) count: a program that leaves them out, or rounds other values in their place, can miss the bound.
Values may be sent and summed in bfloat16 or wider, within the bound.
A program may use at most 64 MiB of HBM per device.

```python
import jax
import jax.numpy as jnp
from jax import lax

C = 512
D = 256
K = 1024
TILE = 2048
TR = 8
TC = 16
H = 256
W = 1024


def draw_tissue_counts(key, part):
    key = jax.random.fold_in(key, 7)
    first_key, second_key = jax.random.split(key)
    tile_rows = jnp.arange(TR, dtype=jnp.int32)[:, None]
    highest = TILE * (tile_rows + 1) // TR
    lowest = highest // 2 + 1
    spread = jax.random.randint(first_key, (TR, TC), 0, 1 << 20, dtype=jnp.int32)
    counts = lowest + spread % (highest - lowest + 1)
    picked = jax.random.randint(second_key, (), 0, TC, dtype=jnp.int32)
    full_tile = (tile_rows == TR - 1) & (jnp.arange(TC, dtype=jnp.int32)[None, :] == picked)
    return jnp.where(full_tile, TILE, counts).astype(jnp.int32)


def shard_levels(stream_key, dims, shards, low, largest):
    def one(axis_at, shards_of):
        steps = jax.random.uniform(jax.random.fold_in(jax.random.fold_in(stream_key, 6), axis_at), (shards_of,), jnp.float32, low / len(shards), largest / len(shards))
        return jnp.repeat(jnp.exp(steps), dims[axis_at] // shards_of).reshape((-1,) + (1,) * (len(dims) - axis_at - 1))

    gain = one(*shards[0])
    for cut in shards[1:]:
        gain = gain * one(*cut)
    return gain


def normal_values(rng, dims, scale, limit, pieces=(), kind=jnp.bfloat16):
    factor_of = shard_levels(rng, dims, pieces, -0.22, 0.18) if pieces else 1.0
    drawn = jax.random.normal(rng, dims, jnp.float32) * scale * factor_of
    return jnp.minimum(jnp.maximum(drawn, -limit), limit).astype(kind)


def setup_inputs(seed: int = 0) -> dict:
    key_of = jax.random.split(jax.random.key(seed), 8)
    features = normal_values(key_of[0], (H, W, C), 1.0, 6.0, ((0, 8), (1, 16)))
    conv_weight = normal_values(key_of[1], (3, 3, C, D), (9 * C) ** -0.5, 0.09375)
    conv_bias = normal_values(key_of[2], (D,), 0.5, 3.0, (), jnp.float32)
    means = normal_values(key_of[3], (K, D), 0.1, 0.6, ((0, 4),), jnp.float32)
    precisions = jnp.clip(1.0 + 0.06 * jax.random.normal(key_of[4], (K, D), jnp.float32), 0.7, 1.3)
    mix_logits = normal_values(key_of[5], (K,), 1.0, 4.0, (), jnp.float32)
    tissue_counts = draw_tissue_counts(jax.random.fold_in(key_of[7], 71), 0)
    return {"features": features, "conv_weight": conv_weight, "conv_bias": conv_bias, "means": means, "precisions": precisions, "mix_logits": mix_logits, "tissue_counts": tissue_counts}


def conv_block(padded, conv_weight, conv_bias, height, width):
    total_sum = jnp.zeros((height * width, conv_weight.shape[3]), jnp.float32)
    for offset_row in range(3):
        for offset_col in range(3):
            window = padded[offset_row:offset_row + height, offset_col:offset_col + width, :].reshape(height * width, padded.shape[2])
            total_sum = total_sum + jnp.dot(window, conv_weight[offset_row, offset_col], preferred_element_type=jnp.float32)
    encoded = (total_sum + conv_bias).astype(jnp.bfloat16)
    widened = encoded.astype(jnp.float32)
    squared = (widened * widened).astype(jnp.bfloat16)
    return jnp.concatenate([encoded, squared], axis=1)

def build_panel(centres, precisions, log_weights):
    panel = jnp.concatenate([(centres * precisions).astype(jnp.bfloat16), (-0.5 * precisions).astype(jnp.bfloat16)], axis=1)
    offset = log_weights + 0.5 * lax.optimization_barrier(jnp.sum(jnp.log(precisions), axis=1)) - 0.5 * lax.optimization_barrier(jnp.sum(precisions * centres * centres, axis=1))
    return (panel, offset)

def score_rows(design, panel, offset):
    return lax.dot_general(design, panel, (((1,), (1,)), ((), ())), preferred_element_type=jnp.float32) + offset

def finish(stats, zeroth, centres, precisions, log_weights, total):
    width = centres.shape[1]
    first = stats[:, :width]
    second = stats[:, width:]
    weights = jnp.exp(log_weights)
    mean_fisher = (first - centres * zeroth[:, None]) * jnp.sqrt(precisions) / jnp.sqrt(total * weights)[:, None]
    var_fisher = (second * precisions - 2.0 * centres * precisions * first + (centres * centres * precisions - 1.0) * zeroth[:, None]) / jnp.sqrt(2.0 * total * weights)[:, None]
    return (mean_fisher, var_fisher)

def reference(features, conv_weight, conv_bias, means, precisions, mix_logits, tissue_counts):
    height_all = features.shape[0]
    width_all = features.shape[1]
    bands = tissue_counts.shape[0]
    across = tissue_counts.shape[1]
    height = height_all // bands
    tile_width = width_all // across
    padded = jnp.pad(features, ((1, 1), (1, 1), (0, 0)))
    log_weights = jax.nn.log_softmax(mix_logits)
    panel, offset = build_panel(means, precisions, log_weights)
    column = jnp.arange(width_all, dtype=jnp.int32)
    inside = jnp.arange(height, dtype=jnp.int32)[:, None] * tile_width + (column % tile_width)[None, :]

    def one_band(band):
        block = lax.dynamic_slice_in_dim(padded, band * height, height + 2, 0)
        design = conv_block(block, conv_weight, conv_bias, height, width_all)
        scores = score_rows(design, panel, offset)
        normal = jax.nn.logsumexp(scores, axis=1)
        limits = tissue_counts[band][column // tile_width]
        valid = (inside < limits[None, :]).reshape(-1).astype(jnp.float32)
        gamma = (jnp.exp(scores - normal[:, None]) * valid[:, None]).astype(jnp.bfloat16)
        stats = lax.dot_general(gamma, design, (((0,), (0,)), ((), ())), preferred_element_type=jnp.float32)
        zeroth = lax.optimization_barrier(jnp.sum(gamma.astype(jnp.float32), axis=0))
        return (stats, zeroth)
    stats_all, zeroth_all = lax.map(one_band, jnp.arange(bands, dtype=jnp.int32))
    total = jnp.sum(tissue_counts).astype(jnp.float32)
    return finish(lax.optimization_barrier(jnp.sum(stats_all, axis=0)), lax.optimization_barrier(jnp.sum(zeroth_all, axis=0)), means, precisions, log_weights, total)
```

```python
import functools

import jax
import jax.numpy as jnp
from jax import lax
from jax.experimental import pallas as pl
from jax.experimental.pallas import tpu as pltpu
from jax.sharding import PartitionSpec as P

F32 = jnp.float32
BF16 = jnp.bfloat16
MESH = pl.DeviceIdType.MESH

HEIGHT, WIDTH, CHAN, DIM = 32, 64, 512, 256
COMPS, BLOCK = 1024, 256
PATCHES = HEIGHT * WIDTH
CHUNK = 512
ROWS = CHUNK // WIDTH
CHIPS = 64
GROUP = 32
LANES = 2 * 128 + 128


def signal(sem, device):
    pl.semaphore_signal(sem, inc=1, device_id=device, device_id_type=MESH)


def remote(src, dst, send_sem, recv_sem, device):
    return pltpu.make_async_remote_copy(
        src_ref=src, dst_ref=dst, send_sem=send_sem, recv_sem=recv_sem,
        device_id=device, device_id_type=MESH,
    )


def column(line):
    return jnp.broadcast_to(line, (128, 128)).T


def kernel(
    features, conv_weight, bias, means, precisions, logits, count, out,
    x, w, sides, corners, edge, panel, offset_lines, offsets, own_logs, design, gamma, zeroth,
    give, take, held, landed, gathered,
    load_sem, halo_send, halo_recv, panel_send, panel_recv, pair_send, pair_recv,
    scatter_send, scatter_recv, gather_send, gather_recv,
):
    row, col, comp = lax.axis_index("row"), lax.axis_index("col"), lax.axis_index("comp")
    core = lax.rem(comp, 2)
    upper = comp // 2
    tile = col * 4 + comp
    me = row * 8 + col * 2 + upper
    partner = (row, col, comp + 1 - 2 * core)
    across = (row + 1 - 2 * lax.rem(row, 2), col, lax.rem(comp + 2, 4))

    def chip(number):
        return (number // 8, lax.rem(number // 2, 4), 2 * lax.rem(number, 2) + core)

    def spot(down, right):
        there = tile + right
        return (row + down, there // 4, lax.rem(there, 4))

    def exists(down, right):
        ok = jnp.bool_(True)
        if down < 0:
            ok = row > 0
        if down > 0:
            ok = row < 7
        if right < 0:
            ok = jnp.logical_and(ok, tile > 0)
        if right > 0:
            ok = jnp.logical_and(ok, tile < 15)
        return ok

    load_x = pltpu.make_async_copy(features, x.at[pl.ds(1, HEIGHT)], load_sem.at[0])
    load_w = pltpu.make_async_copy(conv_weight, w, load_sem.at[1])
    load_x.start()
    load_w.start()

    barrier = pltpu.get_barrier_semaphore()

    def greet(step, carry):
        signal(barrier, chip(lax.rem(me + step, CHIPS)))
        return carry

    lax.fori_loop(1, CHIPS, greet, 0)
    signal(barrier, partner)
    diagonal = [(0, -1), (0, 1), (-1, -1), (-1, 1), (1, -1), (1, 1)]
    greeted = CHIPS
    for place in diagonal:
        @pl.when(exists(*place))
        def _():
            signal(barrier, spot(*place))
        greeted = greeted + exists(*place).astype(jnp.int32)

    centres = means[...]
    inverse = precisions[...]
    panel[comp] = jnp.concatenate(
        [(centres * inverse).astype(BF16), (-0.5 * inverse).astype(BF16)], axis=1
    )
    lines = logits[...]
    top = jnp.max(jnp.max(lines, axis=0), axis=1, keepdims=True)
    norm = top + jnp.log(jnp.sum(jnp.sum(jnp.exp(lines - top[None]), axis=0), axis=1, keepdims=True))
    logs = jnp.concatenate([column(logits[2 * comp] - norm), column(logits[2 * comp + 1] - norm)], axis=0)
    own_logs[...] = logs
    constant = 0.5 * jnp.sum(jnp.log(inverse), axis=1, keepdims=True) - 0.5 * jnp.sum(
        inverse * centres * centres, axis=1, keepdims=True
    )
    own_offset = logs + constant
    for half in range(2):
        offset_lines[comp, half] = own_offset[half * 128 : half * 128 + 128].T[:8]

    pl.semaphore_wait(barrier, greeted)

    def panel_copies(block, slot, device):
        return [
            remote(panel.at[block], panel.at[block], panel_send.at[slot, 0], panel_recv.at[slot, 0], device),
            remote(offset_lines.at[block], offset_lines.at[block], panel_send.at[slot, 1], panel_recv.at[slot, 1], device),
        ]

    far = lax.rem(comp + 2, 4)
    to_across = panel_copies(comp, 0, across)
    to_partner = panel_copies(comp, 1, partner)
    onward = panel_copies(far, 2, partner)

    load_x.wait()
    halos = []

    def halo(index, down, right, src, dst):
        halos.append((index, down, right, remote(src, dst, halo_send.at[index], halo_recv.at[index], spot(down, right))))
        @pl.when(exists(down, right))
        def _():
            halos[-1][3].start()

    halo(0, -1, 0, x.at[1], x.at[HEIGHT + 1])
    halo(1, 1, 0, x.at[HEIGHT], x.at[0])
    halo(2, -1, -1, x.at[1, pl.ds(0, 16)], corners.at[1, 1])
    halo(3, -1, 1, x.at[1, pl.ds(WIDTH - 16, 16)], corners.at[0, 1])
    halo(4, 1, -1, x.at[HEIGHT, pl.ds(0, 16)], corners.at[1, 0])
    halo(5, 1, 1, x.at[HEIGHT, pl.ds(WIDTH - 16, 16)], corners.at[0, 0])
    flat = x[1 : HEIGHT + 1].reshape(PATCHES, CHAN)
    line = lax.broadcasted_iota(jnp.int32, (2 * HEIGHT, PATCHES), 0)
    patch = lax.broadcasted_iota(jnp.int32, (2 * HEIGHT, PATCHES), 1)
    wanted = jnp.where(line < HEIGHT, line * WIDTH, (line - HEIGHT) * WIDTH + WIDTH - 1)
    picked = jnp.dot(
        jnp.where(patch == wanted, 1.0, 0.0).astype(BF16), flat, preferred_element_type=F32
    ).astype(BF16)
    edge[0] = picked[:HEIGHT]
    edge[1] = picked[HEIGHT:]
    halo(6, 0, -1, edge.at[0], sides.at[1])
    halo(7, 0, 1, edge.at[1], sides.at[0])
    for copy in to_across + to_partner:
        copy.start()

    @pl.when(row == 0)
    def _():
        x[0] = jnp.zeros((WIDTH, CHAN), BF16)

    @pl.when(row == 7)
    def _():
        x[HEIGHT + 1] = jnp.zeros((WIDTH, CHAN), BF16)

    for side, edge_tile in ((0, 0), (1, 15)):
        @pl.when(tile == edge_tile)
        def _():
            sides[side] = jnp.zeros((HEIGHT, CHAN), BF16)

        for end, edge_row in ((0, 0), (1, 7)):
            @pl.when(jnp.logical_or(tile == edge_tile, row == edge_row))
            def _():
                corners[side, end] = jnp.zeros((16, CHAN), BF16)

    load_w.wait()
    for index, down, right, copy in halos:
        @pl.when(exists(down, right))
        def _():
            copy.wait_send()

        @pl.when(exists(-down, -right))
        def _():
            copy.wait_recv()

    beside = []
    for side, tap, at in ((0, 0, 15), (1, 2, 0)):
        lhs = jnp.concatenate([sides[side], corners[side, 0], corners[side, 1]], axis=0)
        y = [jnp.dot(lhs, w[k, tap], preferred_element_type=F32) for k in range(3)]
        r = lax.broadcasted_iota(jnp.int32, (HEIGHT, DIM), 0)
        above = jnp.where(r == 0, y[0][32 + at : 33 + at], pltpu.roll(y[0][:HEIGHT], 1, 0))
        below = jnp.where(r == HEIGHT - 1, y[2][48 + at : 49 + at], pltpu.roll(y[2][:HEIGHT], HEIGHT - 1, 0))
        beside.append(above + y[1][:HEIGHT] + below)

    c = lax.broadcasted_iota(jnp.int32, (ROWS, WIDTH, DIM), 1)
    for i in range(PATCHES // CHUNK):
        lhs = jnp.concatenate(
            [x[i * ROWS + k : i * ROWS + k + ROWS].reshape(CHUNK, CHAN) for k in range(3)], axis=1
        )
        y = [
            jnp.dot(lhs, w[:, tap].reshape(3 * CHAN, DIM), preferred_element_type=F32)
            for tap in range(3)
        ]
        left, right = (b[i * ROWS : i * ROWS + ROWS].reshape(ROWS, 1, DIM) for b in beside)
        before = jnp.where(c == 0, left, pltpu.roll(y[0], 1, 0).reshape(ROWS, WIDTH, DIM))
        after = jnp.where(c == WIDTH - 1, right, pltpu.roll(y[2], CHUNK - 1, 0).reshape(ROWS, WIDTH, DIM))
        encoded = (y[1].reshape(ROWS, WIDTH, DIM) + before + after + bias[...].reshape(1, 1, DIM)).reshape(CHUNK, DIM).astype(BF16)
        wide = encoded.astype(F32)
        design[i * CHUNK : (i + 1) * CHUNK, :DIM] = encoded
        design[i * CHUNK : (i + 1) * CHUNK, DIM:] = (wide * wide).astype(BF16)

    for copy in to_across + to_partner:
        copy.wait()
    for copy in onward:
        copy.start()
    for copy in onward:
        copy.wait()
    for block in range(4):
        for half in range(2):
            offsets[block, half * 128 : half * 128 + 128] = column(offset_lines[block, half, :1])

    limit = count[...]
    for i in range(PATCHES // CHUNK):
        flipped = design[i * CHUNK : (i + 1) * CHUNK, :DIM].T
        wide = flipped.astype(F32)
        rhs = jnp.concatenate([flipped, (wide * wide).astype(BF16)], axis=0)
        scores = jnp.dot(panel[...].reshape(COMPS, 2 * DIM), rhs, preferred_element_type=F32)
        scores = scores + jnp.concatenate([offsets[...].reshape(COMPS, 128)] * (CHUNK // 128), axis=1)
        peak = jnp.max(scores, axis=0, keepdims=True)
        mass = jnp.exp(scores - peak)
        where = lax.broadcasted_iota(jnp.int32, (1, CHUNK), 1) + i * CHUNK
        scale = jnp.where(where < limit, 1.0 / jnp.sum(mass, axis=0, keepdims=True), 0.0)
        weight = (mass * scale).astype(BF16)
        gamma[:, i * CHUNK : (i + 1) * CHUNK] = weight
        weight = weight.astype(F32)
        part = weight[:, :128]
        for k in range(1, CHUNK // 128):
            part = part + weight[:, k * 128 : k * 128 + 128]
        if i == 0:
            zeroth[...] = part
        else:
            zeroth[...] += part

    tally = jnp.broadcast_to(limit, (8, 128))
    high = tally // 64
    at = lax.broadcasted_iota(jnp.int32, (8, 128), 0)
    counts = jnp.where(at == 0, high, jnp.where(at == 1, tally - high * 64, 0)).astype(F32)

    def statistics(block):
        rows = pl.ds(pl.multiple_of(block * BLOCK, BLOCK), BLOCK)
        stats = jnp.dot(gamma[rows, :], design[...], preferred_element_type=F32)
        main = jnp.concatenate(
            [stats[:, :DIM].reshape(GROUP, 8, DIM), stats[:, DIM:].reshape(GROUP, 8, DIM)], axis=1
        )
        extra = jnp.concatenate(
            [zeroth[rows, :].reshape(GROUP, 8, 128), jnp.broadcast_to(counts[None], (GROUP, 8, 128))], axis=1
        )
        return jnp.concatenate([main, extra], axis=2)

    pair = []
    for k in range(2):
        give[k] = statistics(2 * k + 1 - core).astype(BF16)
        pair.append(remote(give.at[k], take.at[k], pair_send.at[k], pair_recv.at[k], partner))
        pair[k].start()
    for k in range(2):
        mine = statistics(2 * k + core)
        pair[k].wait()
        held[k] = (mine + take[k].astype(F32)).astype(BF16)

    def scatter(step, carry):
        to = lax.rem(me + step, CHIPS)
        device = chip(to)
        remote(
            held.at[lax.rem(to, 2), to // 2], landed.at[CHIPS - step], scatter_send, scatter_recv, device
        ).start()
        return carry

    lax.fori_loop(1, CHIPS, scatter, 0)
    landed[0] = held[upper, row * 4 + col]
    everyone = remote(landed.at[pl.ds(1, CHIPS - 1)], landed.at[pl.ds(1, CHIPS - 1)], scatter_send, scatter_recv, partner)
    everyone.wait_send()
    everyone.wait_recv()
    total = jnp.sum(landed[...].astype(F32), axis=0)
    first = total[:8, :DIM]
    second = total[8:, :DIM]
    mass = jnp.sum(total[:8, DIM:], axis=1, keepdims=True)
    patches = total[8:9, DIM : DIM + 1] * 64.0 + total[9:10, DIM : DIM + 1]
    owner = row * 4 + col
    rows = pl.ds(pl.multiple_of(owner * 8, 8), 8)
    centre = means[rows, :]
    inverse = precisions[rows, :]
    share = jnp.exp(own_logs[rows, :1])
    mean_fisher = (first - centre * mass) * jnp.sqrt(inverse) / jnp.sqrt(patches * share)
    var_fisher = (
        second * inverse - 2.0 * centre * inverse * first + (centre * centre * inverse - 1.0) * mass
    ) / jnp.sqrt(2.0 * patches * share)
    gathered[owner] = jnp.concatenate([mean_fisher, var_fisher], axis=0).astype(BF16)

    def gather(step, carry):
        to = lax.rem(owner + step, GROUP)
        remote(
            gathered.at[owner], gathered.at[owner], gather_send, gather_recv, (to // 4, lax.rem(to, 4), comp)
        ).start()
        return carry

    lax.fori_loop(1, GROUP, gather, 0)
    others = remote(gathered.at[pl.ds(1, GROUP - 1)], gathered.at[pl.ds(1, GROUP - 1)], gather_send, gather_recv, partner)
    others.wait_send()
    others.wait_recv()
    out[...] = gathered[...]


def shards(features, conv_weight, conv_bias, means, precisions, mix_logits, tissue_counts):
    vmem = pl.BlockSpec(memory_space=pltpu.VMEM)
    anywhere = pl.BlockSpec(memory_space=pl.ANY)
    dma = pltpu.SemaphoreType.DMA
    fisher = pl.pallas_call(
        kernel,
        out_shape=jax.ShapeDtypeStruct((GROUP, 16, DIM), BF16),
        in_specs=[anywhere, anywhere, vmem, vmem, vmem, vmem, vmem],
        out_specs=vmem,
        scratch_shapes=[
            pltpu.VMEM((HEIGHT + 2, WIDTH, CHAN), BF16),
            pltpu.VMEM((3, 3, CHAN, DIM), BF16),
            pltpu.VMEM((2, HEIGHT, CHAN), BF16),
            pltpu.VMEM((2, 2, 16, CHAN), BF16),
            pltpu.VMEM((2, HEIGHT, CHAN), BF16),
            pltpu.VMEM((4, BLOCK, 2 * DIM), BF16),
            pltpu.VMEM((4, 2, 8, 128), F32),
            pltpu.VMEM((4, BLOCK, 128), F32),
            pltpu.VMEM((BLOCK, 128), F32),
            pltpu.VMEM((PATCHES, 2 * DIM), BF16),
            pltpu.VMEM((COMPS, PATCHES), BF16),
            pltpu.VMEM((COMPS, 128), F32),
            pltpu.VMEM((2, GROUP, 16, LANES), BF16),
            pltpu.VMEM((2, GROUP, 16, LANES), BF16),
            pltpu.VMEM((2, GROUP, 16, LANES), BF16),
            pltpu.VMEM((CHIPS, 16, LANES), BF16),
            pltpu.VMEM((GROUP, 16, DIM), BF16),
            dma((2,)), dma((8,)), dma((8,)), dma((3, 2)), dma((3, 2)), dma((2,)), dma((2,)),
            dma, dma, dma, dma,
        ],
        compiler_params=pltpu.CompilerParams(
            collective_id=0, has_side_effects=True, vmem_limit_bytes=48 * 2**20
        ),
    )(
        features, conv_weight, conv_bias.reshape(1, DIM), means, precisions,
        mix_logits.reshape(8, 1, 128), tissue_counts,
    )
    fisher = fisher.astype(F32)
    return (fisher[:, :8].reshape(BLOCK, DIM), fisher[:, 8:].reshape(BLOCK, DIM))


def solution(mesh):
    in_specs = (
        P("row", ("col", "comp"), None),
        P(),
        P(),
        P("comp", None),
        P("comp", None),
        P(),
        P("row", ("col", "comp")),
    )
    out_specs = (P("comp", None), P("comp", None))
    return jax.shard_map(shards, mesh=mesh, in_specs=in_specs, out_specs=out_specs, check_vma=False)
```

```python
import functools

import jax
import jax.numpy as jnp
from jax import lax
from jax.experimental import pallas as pl
from jax.experimental.pallas import tpu as pltpu
from jax.sharding import PartitionSpec as P

F32 = jnp.float32
BF16 = jnp.bfloat16
MESH = pl.DeviceIdType.MESH

HEIGHT, WIDTH, CHAN, DIM = 32, 64, 512, 256
COMPS, BLOCK = 1024, 256
PATCHES = HEIGHT * WIDTH
CHUNK = 512
ROWS = CHUNK // WIDTH
CHIPS = 64
GROUP = 32
PIECES = 4


def signal(sem, device):
    pl.semaphore_signal(sem, inc=1, device_id=device, device_id_type=MESH)


def remote(src, dst, send_sem, recv_sem, device):
    return pltpu.make_async_remote_copy(
        src_ref=src, dst_ref=dst, send_sem=send_sem, recv_sem=recv_sem,
        device_id=device, device_id_type=MESH,
    )


def column(line):
    return jnp.broadcast_to(line, (128, 128)).T


def kernel(
    features, conv_weight, bias_in, means_in, precisions_in, logits_in, count_in, out,
    x, w, bias, logits, count, means, precisions, ends, raw, sides, corners, edge, panel, offset_lines, offsets,
    own_logs, design, mass, gamma, zeroth, give, take, held, landed, gathered,
    sums_give, sums_take, sums_held, sums_landed, sums_column,
    load_sem, halo_send, halo_recv, panel_send, panel_recv, pair_send, pair_recv,
    sums_pair, scatter_send, scatter_recv, sums_send, sums_recv, gather_send, gather_recv, heard,
):
    row, col, comp = lax.axis_index("row"), lax.axis_index("col"), lax.axis_index("comp")
    core = lax.rem(comp, 2)
    upper = comp // 2
    tile = col * 4 + comp
    me = row * 8 + col * 2 + upper
    partner = (row, col, comp + 1 - 2 * core)
    across = (row + 1 - 2 * lax.rem(row, 2), col, lax.rem(comp + 2, 4))

    def chip(number):
        return (number // 8, lax.rem(number // 2, 4), 2 * lax.rem(number, 2) + core)

    def spot(down, right):
        there = tile + right
        return (row + down, there // 4, lax.rem(there, 4))

    def exists(down, right):
        ok = jnp.bool_(True)
        if down < 0:
            ok = row > 0
        if down > 0:
            ok = row < 7
        if right < 0:
            ok = jnp.logical_and(ok, tile > 0)
        if right > 0:
            ok = jnp.logical_and(ok, tile < 15)
        return ok

    loads = [
        pltpu.make_async_copy(src, dst, load_sem.at[k])
        for k, (src, dst) in enumerate((
            (means_in, means), (precisions_in, precisions), (features, x.at[pl.ds(1, HEIGHT)]), (logits_in, logits),
            (bias_in, bias), (count_in, count), (conv_weight, w),
        ))
    ]
    for load in loads:
        load.start()

    barrier = pltpu.get_barrier_semaphore()
    lower = lax.rem(row, 2)
    z_peers = [(row, lax.rem(col + k, 4), comp) for k in (1, 2, 3)]
    x_peers = [(lax.rem(row + 2 * k, 8), col, comp) for k in (1, 2, 3)]
    y_peers = [
        (row + 1 - 2 * lower, col, comp),
        (row, col, lax.rem(comp + 2, 4)),
        across,
    ]
    around = [(-1, 0), (1, 0), (0, -1), (0, 1), (-1, -1), (-1, 1), (1, -1), (1, 1)]
    for device in y_peers + [partner] + x_peers + z_peers:
        signal(barrier, device)
    greeted = 10
    for place in around:
        @pl.when(exists(*place))
        def _():
            signal(barrier, spot(*place))
        greeted = greeted + exists(*place).astype(jnp.int32)

    loads[0].wait()
    loads[1].wait()
    centres = means[...]
    inverse = precisions[...]
    panel[comp] = jnp.concatenate(
        [(centres * inverse).astype(BF16), (-0.5 * inverse).astype(BF16)], axis=1
    )
    pl.semaphore_wait(barrier, greeted)

    def hear(peers, k):
        for device in peers:
            signal(heard.at[k], device)

    far = lax.rem(comp + 2, 4)
    beyond = far + 1 - 2 * core

    def panel_copy(block, piece, slot, device):
        rows = panel.at[block, pl.ds(piece * (BLOCK // PIECES), BLOCK // PIECES)]
        return remote(rows, rows, panel_send.at[slot, piece], panel_recv.at[slot, piece], device)

    def offset_copy(block, slot, device):
        lines = offset_lines.at[block]
        return remote(lines, lines, panel_send.at[slot, PIECES], panel_recv.at[slot, PIECES], device)

    to_across = [panel_copy(comp, piece, 0, across) for piece in range(PIECES)]
    to_partner = [panel_copy(comp, piece, 1, partner) for piece in range(PIECES)]
    onward = [panel_copy(far, piece, 2, partner) for piece in range(PIECES)]
    offsets_across, offsets_partner, offsets_onward = (
        offset_copy(comp, 0, across), offset_copy(comp, 1, partner), offset_copy(far, 2, partner)
    )
    for copy in to_across + to_partner:
        copy.start()
    hear(x_peers, 0)

    loads[2].wait()
    halos = []

    def halo(index, down, right, src, dst):
        halos.append((index, down, right, remote(src, dst, halo_send.at[index], halo_recv.at[index], spot(down, right))))
        @pl.when(exists(down, right))
        def _():
            halos[-1][3].start()

    halo(0, -1, 0, x.at[1], ends.at[1])
    halo(1, 1, 0, x.at[HEIGHT], ends.at[0])
    halo(2, -1, -1, x.at[1, pl.ds(0, 16)], corners.at[1, 1])
    halo(3, -1, 1, x.at[1, pl.ds(WIDTH - 16, 16)], corners.at[0, 1])
    halo(4, 1, -1, x.at[HEIGHT, pl.ds(0, 16)], corners.at[1, 0])
    halo(5, 1, 1, x.at[HEIGHT, pl.ds(WIDTH - 16, 16)], corners.at[0, 0])
    flat = x[1 : HEIGHT + 1].reshape(PATCHES, CHAN)
    line = lax.broadcasted_iota(jnp.int32, (2 * HEIGHT, PATCHES), 0)
    patch = lax.broadcasted_iota(jnp.int32, (2 * HEIGHT, PATCHES), 1)
    wanted = jnp.where(line < HEIGHT, line * WIDTH, (line - HEIGHT) * WIDTH + WIDTH - 1)
    picked = jnp.dot(
        jnp.where(patch == wanted, 1.0, 0.0).astype(BF16), flat, preferred_element_type=F32
    ).astype(BF16)
    edge[0] = picked[:HEIGHT]
    edge[1] = picked[HEIGHT:]
    halo(6, 0, -1, edge.at[0], sides.at[1])
    halo(7, 0, 1, edge.at[1], sides.at[0])

    loads[3].wait()
    lines = logits[...]
    top = jnp.max(jnp.max(lines, axis=0), axis=1, keepdims=True)
    norm = top + jnp.log(jnp.sum(jnp.sum(jnp.exp(lines - top[None]), axis=0), axis=1, keepdims=True))
    logs = jnp.concatenate([column(logits[2 * comp] - norm), column(logits[2 * comp + 1] - norm)], axis=0)
    own_logs[...] = logs
    constant = 0.5 * jnp.sum(jnp.log(inverse), axis=1, keepdims=True) - 0.5 * jnp.sum(
        inverse * centres * centres, axis=1, keepdims=True
    )
    own_offset = logs + constant
    for half in range(2):
        offset_lines[comp, half] = own_offset[half * 128 : half * 128 + 128].T[:8]
    offsets_across.start()
    offsets_partner.start()

    x[0] = jnp.zeros((WIDTH, CHAN), BF16)
    x[HEIGHT + 1] = jnp.zeros((WIDTH, CHAN), BF16)

    @pl.when(row == 0)
    def _():
        ends[0] = jnp.zeros((WIDTH, CHAN), BF16)

    @pl.when(row == 7)
    def _():
        ends[1] = jnp.zeros((WIDTH, CHAN), BF16)

    for side, edge_tile in ((0, 0), (1, 15)):
        @pl.when(tile == edge_tile)
        def _():
            sides[side] = jnp.zeros((HEIGHT, CHAN), BF16)

        for end, edge_row in ((0, 0), (1, 7)):
            @pl.when(jnp.logical_or(tile == edge_tile, row == edge_row))
            def _():
                corners[side, end] = jnp.zeros((16, CHAN), BF16)

    for load in loads[4:]:
        load.wait()

    def shifted(y, height):
        c = lax.broadcasted_iota(jnp.int32, (height, WIDTH, DIM), 1)
        count = height * WIDTH
        before = jnp.where(c == 0, 0.0, pltpu.roll(y[0], 1, 0).reshape(height, WIDTH, DIM))
        after = jnp.where(c == WIDTH - 1, 0.0, pltpu.roll(y[2], count - 1, 0).reshape(height, WIDTH, DIM))
        return y[1].reshape(height, WIDTH, DIM) + before + after

    def convolve(i):
        lhs = jnp.concatenate(
            [x[i * ROWS + k : i * ROWS + k + ROWS].reshape(CHUNK, CHAN) for k in range(3)], axis=1
        )
        y = [
            jnp.dot(lhs, w[:, tap].reshape(3 * CHAN, DIM), preferred_element_type=F32)
            for tap in range(3)
        ]
        raw[i * ROWS : (i + 1) * ROWS] = shifted(y, ROWS) + bias[...].reshape(1, 1, DIM)

    for i in range(PATCHES // CHUNK):
        convolve(i)

    pl.semaphore_wait(heard.at[0], 3)
    hear(y_peers, 1)
    for index, down, right, copy in halos:
        @pl.when(exists(down, right))
        def _():
            copy.wait_send()

        @pl.when(exists(-down, -right))
        def _():
            copy.wait_recv()

    beside = [jnp.concatenate([sides[side], corners[side, 0], corners[side, 1]], axis=0) for side in range(2)]
    products = {}
    for k in range(3):
        for tap in range(3):
            lhs = []
            if k != 1:
                lhs.append(ends[k // 2])
            if tap != 1:
                lhs.append(beside[tap // 2])
            if lhs:
                products[k, tap] = jnp.dot(
                    lhs[0] if len(lhs) == 1 else jnp.concatenate(lhs, axis=0), w[k, tap], preferred_element_type=F32
                )
    for k, at in ((0, 0), (2, HEIGHT - 1)):
        raw[at] += shifted([products[k, tap][:WIDTH] for tap in range(3)], 1)[0]
    r = lax.broadcasted_iota(jnp.int32, (HEIGHT, DIM), 0)
    c = lax.broadcasted_iota(jnp.int32, (HEIGHT, 8, DIM), 1)
    for side, tap, at in ((0, 0, 15), (1, 2, 0)):
        y = [products[k, tap][-WIDTH:] for k in range(3)]
        above = jnp.where(r == 0, y[0][32 + at : 33 + at], pltpu.roll(y[0][:HEIGHT], 1, 0))
        below = jnp.where(r == HEIGHT - 1, y[2][48 + at : 49 + at], pltpu.roll(y[2][:HEIGHT], HEIGHT - 1, 0))
        more = (above + y[1][:HEIGHT] + below).reshape(HEIGHT, 1, DIM)
        if side == 0:
            raw[:, :8] += jnp.where(c == 0, more, 0.0)
        else:
            raw[:, WIDTH - 8 :] += jnp.where(c == 7, more, 0.0)

    for i in range(PATCHES // CHUNK):
        encoded = raw[i * ROWS : (i + 1) * ROWS].reshape(CHUNK, DIM).astype(BF16)
        wide = encoded.astype(F32)
        design[i * CHUNK : (i + 1) * CHUNK, :DIM] = encoded
        design[i * CHUNK : (i + 1) * CHUNK, DIM:] = (wide * wide).astype(BF16)

    offsets_across.wait()
    offsets_onward.start()
    for piece in range(2):
        to_across[piece].wait()
        onward[piece].start()

    for copy in to_partner + [offsets_partner]:
        copy.wait()

    def score(i, first, second):
        flipped = design[i * CHUNK : (i + 1) * CHUNK, :DIM].T
        wide = flipped.astype(F32)
        rhs = jnp.concatenate([flipped, (wide * wide).astype(BF16)], axis=0)
        lhs = jnp.concatenate([panel[first], panel[second]], axis=0)
        add = jnp.concatenate([offsets[first], offsets[second]], axis=0)
        scores = jnp.dot(lhs, rhs, preferred_element_type=F32) + jnp.concatenate([add] * (CHUNK // 128), axis=1)
        peak = jnp.max(scores, axis=0, keepdims=True)
        grown = jnp.exp(scores - peak)
        return peak, grown, jnp.sum(grown, axis=0, keepdims=True)

    def spread_offsets(block):
        for half in range(2):
            offsets[block, half * 128 : half * 128 + 128] = column(offset_lines[block, half, :1])

    spread_offsets(comp)
    spread_offsets(comp + 1 - 2 * core)
    near = []
    for i in range(PATCHES // CHUNK):
        peak, grown, total = score(i, comp, comp + 1 - 2 * core)
        mass[:, i * CHUNK : (i + 1) * CHUNK] = grown
        near.append((peak, total))

    for piece in range(2, PIECES):
        to_across[piece].wait()
        onward[piece].start()
    for copy in [offsets_onward] + onward:
        copy.wait()
    spread_offsets(far)
    spread_offsets(beyond)
    limit = count[...]
    for i in range(PATCHES // CHUNK):
        at = slice(i * CHUNK, (i + 1) * CHUNK)
        peak, grown, total = score(i, far, beyond)
        near_peak, near_total = near[i]
        top = jnp.maximum(peak, near_peak)
        lift, near_lift = jnp.exp(peak - top), jnp.exp(near_peak - top)
        where = lax.broadcasted_iota(jnp.int32, (1, CHUNK), 1) + i * CHUNK
        scale = jnp.where(where < limit, 1.0 / (total * lift + near_total * near_lift), 0.0)
        for k, weight in ((0, mass[:, at] * (scale * near_lift)), (1, grown * (scale * lift))):
            rows = slice(k * 512, (k + 1) * 512)
            weight = weight.astype(BF16)
            gamma[rows, at] = weight
            weight = weight.astype(F32)
            part = weight[:, :128]
            for m in range(1, CHUNK // 128):
                part = part + weight[:, m * 128 : m * 128 + 128]
            if i == 0:
                zeroth[rows] = part
            else:
                zeroth[rows] += part

    pl.semaphore_wait(heard.at[1], 3)

    tally = jnp.broadcast_to(limit.astype(F32), (1, 128))
    for h, order in ((0, 0), (1, 2)):
        for half in range(2):
            for ref, place in ((sums_held, order), (sums_give, order + 1)):
                start = place * BLOCK + half * 128
                ref[h, half, 0] = jnp.sum(zeroth[start : start + 128].T, axis=0, keepdims=True)
                ref[h, half, 1] = tally
    sums_copy = remote(sums_give, sums_take, sums_pair.at[0], sums_pair.at[1], partner)
    sums_copy.start()

    def statistics(place):
        stats = jnp.dot(gamma[place * BLOCK : (place + 1) * BLOCK, :], design[...], preferred_element_type=F32)
        return jnp.concatenate(
            [stats[:, :DIM].reshape(GROUP, 8, DIM), stats[:, DIM:].reshape(GROUP, 8, DIM)], axis=1
        )

    pair = []
    for k in range(2):
        give[k] = statistics(2 * k + 1).astype(BF16)
        pair.append(remote(give.at[k], take.at[k], pair_send.at[k], pair_recv.at[k], partner))
        pair[k].start()

    sums_copy.wait()
    sums_held[...] += sums_take[...]

    def scatter(k):
        def send(step, carry):
            step = 2 * step + k
            to = lax.rem(me + step, CHIPS)
            remote(held.at[k, to // 2], landed.at[CHIPS - step], scatter_send, scatter_recv, chip(to)).start()
            return carry

        lax.fori_loop(1 - k, GROUP, send, 0)

    def scatter_sums(step, carry):
        to = lax.rem(me + step, CHIPS)
        away = lax.rem(lax.rem(to, 2) + upper, 2)
        remote(
            sums_held.at[away, to // 32], sums_landed.at[CHIPS - step], sums_send, sums_recv, chip(to)
        ).start()
        return carry

    for k in range(2):
        mine = statistics(2 * k)
        pair[k].wait()
        held[k] = (mine + take[k].astype(F32)).astype(BF16)
        scatter(k)
        if k == 0:
            lax.fori_loop(1, CHIPS, scatter_sums, 0)

    owner = row * 4 + col
    landed[0] = held[0, owner]
    sums_landed[0] = sums_held[0, owner // 16]
    for buffer, send, recv in ((sums_landed, sums_send, sums_recv), (landed, scatter_send, scatter_recv)):
        all_but_own = buffer.at[pl.ds(1, CHIPS - 1)]
        everyone = remote(all_but_own, all_but_own, send, recv, partner)
        everyone.wait_send()
        everyone.wait_recv()
    sums = jnp.sum(sums_landed[...], axis=0)
    sums_column[...] = column(sums[0])
    patches = sums[1][:, :1]
    total = jnp.sum(landed[...].astype(F32), axis=0)
    first = total[:8]
    second = total[8:]
    amount = sums_column[pl.ds(pl.multiple_of(lax.rem(owner, 16) * 8, 8), 8), :]
    amount = jnp.concatenate([amount, amount], axis=1)
    rows = pl.ds(pl.multiple_of(owner * 8, 8), 8)
    centre = means[rows, :]
    inverse = precisions[rows, :]
    share = jnp.exp(own_logs[rows, :1])
    mean_fisher = (first - centre * amount) * jnp.sqrt(inverse) / jnp.sqrt(patches * share)
    var_fisher = (
        second * inverse - 2.0 * centre * inverse * first + (centre * centre * inverse - 1.0) * amount
    ) / jnp.sqrt(2.0 * patches * share)
    gathered[owner] = jnp.concatenate([mean_fisher, var_fisher], axis=0).astype(BF16)

    def gather(step, carry):
        to = lax.rem(owner + step, GROUP)
        remote(
            gathered.at[owner], gathered.at[owner], gather_send, gather_recv, (to // 4, lax.rem(to, 4), comp)
        ).start()
        return carry

    lax.fori_loop(1, GROUP, gather, 0)
    others = remote(gathered.at[pl.ds(1, GROUP - 1)], gathered.at[pl.ds(1, GROUP - 1)], gather_send, gather_recv, partner)
    others.wait_send()
    others.wait_recv()
    out[...] = gathered[...]


def shards(features, conv_weight, conv_bias, means, precisions, mix_logits, tissue_counts):
    vmem = pl.BlockSpec(memory_space=pltpu.VMEM)
    hbm = pl.BlockSpec(memory_space=pltpu.HBM)
    dma = pltpu.SemaphoreType.DMA
    fisher = pl.pallas_call(
        kernel,
        out_shape=jax.ShapeDtypeStruct((GROUP, 16, DIM), BF16),
        in_specs=[hbm] * 7,
        out_specs=vmem,
        scratch_shapes=[
            pltpu.VMEM((HEIGHT + 2, WIDTH, CHAN), BF16),
            pltpu.VMEM((3, 3, CHAN, DIM), BF16),
            pltpu.VMEM((1, DIM), F32),
            pltpu.VMEM((8, 1, 128), F32),
            pltpu.VMEM((1, 1), jnp.int32),
            pltpu.VMEM((BLOCK, DIM), F32),
            pltpu.VMEM((BLOCK, DIM), F32),
            pltpu.VMEM((2, WIDTH, CHAN), BF16),
            pltpu.VMEM((HEIGHT, WIDTH, DIM), F32),
            pltpu.VMEM((2, HEIGHT, CHAN), BF16),
            pltpu.VMEM((2, 2, 16, CHAN), BF16),
            pltpu.VMEM((2, HEIGHT, CHAN), BF16),
            pltpu.VMEM((4, BLOCK, 2 * DIM), BF16),
            pltpu.VMEM((4, 2, 8, 128), F32),
            pltpu.VMEM((4, BLOCK, 128), F32),
            pltpu.VMEM((BLOCK, 128), F32),
            pltpu.VMEM((PATCHES, 2 * DIM), BF16),
            pltpu.VMEM((COMPS // 2, PATCHES), F32),
            pltpu.VMEM((COMPS, PATCHES), BF16),
            pltpu.VMEM((COMPS, 128), F32),
            pltpu.VMEM((2, GROUP, 16, DIM), BF16),
            pltpu.VMEM((2, GROUP, 16, DIM), BF16),
            pltpu.VMEM((2, GROUP, 16, DIM), BF16),
            pltpu.VMEM((CHIPS, 16, DIM), BF16),
            pltpu.VMEM((GROUP, 16, DIM), BF16),
            pltpu.VMEM((2, 2, 2, 1, 128), F32),
            pltpu.VMEM((2, 2, 2, 1, 128), F32),
            pltpu.VMEM((2, 2, 2, 1, 128), F32),
            pltpu.VMEM((CHIPS, 2, 1, 128), F32),
            pltpu.VMEM((128, 128), F32),
            dma((7,)), dma((8,)), dma((8,)), dma((3, PIECES + 1)), dma((3, PIECES + 1)), dma((2,)), dma((2,)),
            dma((2,)), dma, dma, dma, dma, dma, dma, pltpu.SemaphoreType.REGULAR((2,)),
        ],
        compiler_params=pltpu.CompilerParams(
            collective_id=0, has_side_effects=True, vmem_limit_bytes=56 * 2**20
        ),
    )(
        features, conv_weight, conv_bias.reshape(1, DIM), means, precisions,
        mix_logits.reshape(8, 1, 128), tissue_counts,
    )
    return tuple(
        fisher[:, 8 * k : 8 * k + 8].astype(F32).reshape(BLOCK, DIM) for k in range(2)
    )


def solution(mesh):
    in_specs = (
        P("row", ("col", "comp"), None),
        P(),
        P(),
        P("comp", None),
        P("comp", None),
        P(),
        P("row", ("col", "comp")),
    )
    out_specs = (P("comp", None), P("comp", None))
    return jax.shard_map(shards, mesh=mesh, in_specs=in_specs, out_specs=out_specs, check_vma=False)
```

```python
import functools

import jax
import jax.numpy as jnp
from jax import lax
from jax.experimental import pallas as pl
from jax.experimental.pallas import tpu as pltpu
from jax.sharding import PartitionSpec as P

F32 = jnp.float32
BF16 = jnp.bfloat16
MESH = pl.DeviceIdType.MESH

HEIGHT, WIDTH, CHAN, DIM = 32, 64, 512, 256
COMPS, BLOCK = 1024, 256
PATCHES = HEIGHT * WIDTH
CHUNK = 512
ROWS = CHUNK // WIDTH
CHIPS = 64
GROUP = 32
PIECES = 4


def signal(sem, device):
    pl.semaphore_signal(sem, inc=1, device_id=device, device_id_type=MESH)


def remote(src, dst, send_sem, recv_sem, device):
    return pltpu.make_async_remote_copy(
        src_ref=src, dst_ref=dst, send_sem=send_sem, recv_sem=recv_sem,
        device_id=device, device_id_type=MESH,
    )


def column(line):
    return jnp.broadcast_to(line, (128, 128)).T


def kernel(
    features, conv_weight, bias_in, means_in, precisions_in, logits_in, count_in, out,
    x, w, bias, logits, count, means, precisions, ends, raw, sides, corners, corners_out, edge, panel, offset_lines, offsets,
    own_logs, design, mass, gamma, zeroth, give, take, held, landed, gathered,
    sums_give, sums_take, sums_held, sums_landed, sums_total, sums_column,
    load_sem, halo_send, halo_recv, panel_send, panel_recv, pair_send, pair_recv,
    sums_pair, scatter_send, scatter_recv, sums_send, sums_recv, gather_send, gather_recv, total_send, total_recv, heard,
):
    row, col, comp = lax.axis_index("row"), lax.axis_index("col"), lax.axis_index("comp")
    core = lax.rem(comp, 2)
    upper = comp // 2
    tile = col * 4 + comp
    me = row * 8 + col * 2 + upper
    partner = (row, col, comp + 1 - 2 * core)
    across = (row + 1 - 2 * lax.rem(row, 2), col, lax.rem(comp + 2, 4))

    def chip(number):
        return (number // 8, lax.rem(number // 2, 4), 2 * lax.rem(number, 2) + core)

    def spot(down, right):
        there = tile + right
        return (row + down, there // 4, lax.rem(there, 4))

    def exists(down, right):
        ok = jnp.bool_(True)
        if down < 0:
            ok = row > 0
        if down > 0:
            ok = row < 7
        if right < 0:
            ok = jnp.logical_and(ok, tile > 0)
        if right > 0:
            ok = jnp.logical_and(ok, tile < 15)
        return ok

    loads = [
        pltpu.make_async_copy(src, dst, load_sem.at[k])
        for k, (src, dst) in enumerate((
            (means_in, means), (precisions_in, precisions), (features, x.at[pl.ds(1, HEIGHT)]), (logits_in, logits),
            (bias_in, bias), (count_in, count), (conv_weight, w),
        ))
    ]
    for load in loads:
        load.start()

    barrier = pltpu.get_barrier_semaphore()
    lower = lax.rem(row, 2)
    z_peers = [(row, lax.rem(col + k, 4), comp) for k in (1, 2, 3)]
    x_peers = [(lax.rem(row + 2 * k, 8), col, comp) for k in (1, 2, 3)]
    y_peers = [
        (row + 1 - 2 * lower, col, comp),
        (row, col, lax.rem(comp + 2, 4)),
        across,
    ]
    around = [(-1, 0), (1, 0), (0, -1), (0, 1), (-1, -1), (-1, 1), (1, -1), (1, 1)]
    for device in y_peers + [partner] + x_peers + z_peers:
        signal(barrier, device)
    greeted = 10
    for place in around:
        @pl.when(exists(*place))
        def _():
            signal(barrier, spot(*place))
        greeted = greeted + exists(*place).astype(jnp.int32)

    loads[0].wait()
    loads[1].wait()
    centres = means[...]
    inverse = precisions[...]
    panel[comp] = jnp.concatenate(
        [(centres * inverse).astype(BF16), (-0.5 * inverse).astype(BF16)], axis=1
    )
    pl.semaphore_wait(barrier, greeted)

    def hear(peers, k):
        for device in peers:
            signal(heard.at[k], device)

    far = lax.rem(comp + 2, 4)
    beyond = far + 1 - 2 * core

    def panel_copy(block, piece, slot, device):
        rows = panel.at[block, pl.ds(piece * (BLOCK // PIECES), BLOCK // PIECES)]
        return remote(rows, rows, panel_send.at[slot, piece], panel_recv.at[slot, piece], device)

    def offset_copy(block, slot, device):
        lines = offset_lines.at[block]
        return remote(lines, lines, panel_send.at[slot, PIECES], panel_recv.at[slot, PIECES], device)

    to_across = [panel_copy(comp, piece, 0, across) for piece in range(PIECES)]
    to_partner = [panel_copy(comp, piece, 1, partner) for piece in range(PIECES)]
    onward = [panel_copy(far, piece, 2, partner) for piece in range(PIECES)]
    offsets_across, offsets_partner, offsets_onward = (
        offset_copy(comp, 0, across), offset_copy(comp, 1, partner), offset_copy(far, 2, partner)
    )
    for copy in to_across + to_partner:
        copy.start()
    hear(x_peers, 0)

    loads[2].wait()
    halos = []

    def halo(index, down, right, src, dst):
        halos.append((index, down, right, remote(src, dst, halo_send.at[index], halo_recv.at[index], spot(down, right))))
        @pl.when(exists(down, right))
        def _():
            halos[-1][3].start()

    halo(0, -1, 0, x.at[1], ends.at[1])
    halo(1, 1, 0, x.at[HEIGHT], ends.at[0])
    flat = x[1 : HEIGHT + 1].reshape(PATCHES, CHAN)
    line = lax.broadcasted_iota(jnp.int32, (2 * HEIGHT, PATCHES), 0)
    patch = lax.broadcasted_iota(jnp.int32, (2 * HEIGHT, PATCHES), 1)
    wanted = jnp.where(line < HEIGHT, line * WIDTH, (line - HEIGHT) * WIDTH + WIDTH - 1)
    picked = jnp.dot(
        jnp.where(patch == wanted, 1.0, 0.0).astype(BF16), flat, preferred_element_type=F32
    ).astype(BF16)
    edge[0] = picked[:HEIGHT]
    edge[1] = picked[HEIGHT:]
    halo(6, 0, -1, edge.at[0], sides.at[1])
    halo(7, 0, 1, edge.at[1], sides.at[0])
    for index, down, right in ((2, -1, -1), (3, -1, 1), (4, 1, -1), (5, 1, 1)):
        side, end = (1 - right) // 2, (1 - down) // 2
        k = 0 if down < 0 else HEIGHT - 1
        spread = picked[(1 - side) * HEIGHT + k : (1 - side) * HEIGHT + k + 1].astype(F32)
        spread = jnp.concatenate(
            [spread[:, 128 * q : 128 * q + 128] for q in range(4)] + [jnp.zeros((12, 128), F32)], axis=0
        )
        corners_out[side, end] = spread.astype(BF16)
        halo(index, down, right, corners_out.at[side, end], corners.at[side, end])

    loads[3].wait()
    lines = logits[...]
    top = jnp.max(jnp.max(lines, axis=0), axis=1, keepdims=True)
    norm = top + jnp.log(jnp.sum(jnp.sum(jnp.exp(lines - top[None]), axis=0), axis=1, keepdims=True))
    logs = jnp.concatenate([column(logits[2 * comp] - norm), column(logits[2 * comp + 1] - norm)], axis=0)
    own_logs[...] = logs
    constant = 0.5 * jnp.sum(jnp.log(inverse), axis=1, keepdims=True) - 0.5 * jnp.sum(
        inverse * centres * centres, axis=1, keepdims=True
    )
    own_offset = logs + constant
    for half in range(2):
        offset_lines[comp, half] = own_offset[half * 128 : half * 128 + 128].T[:8]
    offsets_across.start()
    offsets_partner.start()

    x[0] = jnp.zeros((WIDTH, CHAN), BF16)
    x[HEIGHT + 1] = jnp.zeros((WIDTH, CHAN), BF16)

    @pl.when(row == 0)
    def _():
        ends[0] = jnp.zeros((WIDTH, CHAN), BF16)

    @pl.when(row == 7)
    def _():
        ends[1] = jnp.zeros((WIDTH, CHAN), BF16)

    for side, edge_tile in ((0, 0), (1, 15)):
        @pl.when(tile == edge_tile)
        def _():
            sides[side] = jnp.zeros((HEIGHT, CHAN), BF16)

        for end, edge_row in ((0, 0), (1, 7)):
            @pl.when(jnp.logical_or(tile == edge_tile, row == edge_row))
            def _():
                corners[side, end] = jnp.zeros((16, 128), BF16)

    for load in loads[4:]:
        load.wait()

    def shifted(y, height):
        c = lax.broadcasted_iota(jnp.int32, (height, WIDTH, DIM), 1)
        count = height * WIDTH
        before = jnp.where(c == 0, 0.0, pltpu.roll(y[0], 1, 0).reshape(height, WIDTH, DIM))
        after = jnp.where(c == WIDTH - 1, 0.0, pltpu.roll(y[2], count - 1, 0).reshape(height, WIDTH, DIM))
        return y[1].reshape(height, WIDTH, DIM) + before + after

    def convolve(i):
        lhs = jnp.concatenate(
            [x[i * ROWS + k : i * ROWS + k + ROWS].reshape(CHUNK, CHAN) for k in range(3)], axis=1
        )
        y = [
            jnp.dot(lhs, w[:, tap].reshape(3 * CHAN, DIM), preferred_element_type=F32)
            for tap in range(3)
        ]
        raw[i * ROWS : (i + 1) * ROWS] = shifted(y, ROWS) + bias[...].reshape(1, 1, DIM)

    for i in range(PATCHES // CHUNK):
        convolve(i)

    pl.semaphore_wait(heard.at[0], 3)
    hear(y_peers, 1)
    for index, down, right, copy in halos:
        @pl.when(exists(down, right))
        def _():
            copy.wait_send()

        @pl.when(exists(-down, -right))
        def _():
            copy.wait_recv()

    def corner(side, end):
        tile_of = corners[side, end].astype(F32)
        line = jnp.concatenate([tile_of[q : q + 1] for q in range(4)], axis=1)
        return jnp.broadcast_to(line, (16, CHAN)).astype(BF16)

    beside = [jnp.concatenate([sides[side], corner(side, 0), corner(side, 1)], axis=0) for side in range(2)]
    products = {}
    for k in range(3):
        for tap in range(3):
            lhs = []
            if k != 1:
                lhs.append(ends[k // 2])
            if tap != 1:
                lhs.append(beside[tap // 2])
            if lhs:
                products[k, tap] = jnp.dot(
                    lhs[0] if len(lhs) == 1 else jnp.concatenate(lhs, axis=0), w[k, tap], preferred_element_type=F32
                )
    for k, at in ((0, 0), (2, HEIGHT - 1)):
        raw[at] += shifted([products[k, tap][:WIDTH] for tap in range(3)], 1)[0]
    r = lax.broadcasted_iota(jnp.int32, (HEIGHT, DIM), 0)
    c = lax.broadcasted_iota(jnp.int32, (HEIGHT, 8, DIM), 1)
    for side, tap in ((0, 0), (1, 2)):
        y = [products[k, tap][-WIDTH:] for k in range(3)]
        above = jnp.where(r == 0, y[0][32:33], pltpu.roll(y[0][:HEIGHT], 1, 0))
        below = jnp.where(r == HEIGHT - 1, y[2][48:49], pltpu.roll(y[2][:HEIGHT], HEIGHT - 1, 0))
        more = (above + y[1][:HEIGHT] + below).reshape(HEIGHT, 1, DIM)
        if side == 0:
            raw[:, :8] += jnp.where(c == 0, more, 0.0)
        else:
            raw[:, WIDTH - 8 :] += jnp.where(c == 7, more, 0.0)

    for i in range(PATCHES // CHUNK):
        encoded = raw[i * ROWS : (i + 1) * ROWS].reshape(CHUNK, DIM).astype(BF16)
        wide = encoded.astype(F32)
        design[i * CHUNK : (i + 1) * CHUNK, :DIM] = encoded
        design[i * CHUNK : (i + 1) * CHUNK, DIM:] = (wide * wide).astype(BF16)

    for copy in to_partner + [offsets_partner]:
        copy.wait()

    def score(i, first, second):
        flipped = design[i * CHUNK : (i + 1) * CHUNK, :DIM].T
        wide = flipped.astype(F32)
        rhs = jnp.concatenate([flipped, (wide * wide).astype(BF16)], axis=0)
        lhs = jnp.concatenate([panel[first], panel[second]], axis=0)
        add = jnp.concatenate([offsets[first], offsets[second]], axis=0)
        scores = jnp.dot(lhs, rhs, preferred_element_type=F32) + jnp.concatenate([add] * (CHUNK // 128), axis=1)
        peak = jnp.max(scores, axis=0, keepdims=True)
        grown = jnp.exp(scores - peak)
        return peak, grown, jnp.sum(grown, axis=0, keepdims=True)

    def spread_offsets(block):
        for half in range(2):
            offsets[block, half * 128 : half * 128 + 128] = column(offset_lines[block, half, :1])

    spread_offsets(comp)
    spread_offsets(comp + 1 - 2 * core)
    near = []
    for i in range(PATCHES // CHUNK):
        peak, grown, total = score(i, comp, comp + 1 - 2 * core)
        mass[:, i * CHUNK : (i + 1) * CHUNK] = grown
        near.append((peak, total))
        if i >= 1:
            to_across[i - 1].wait()
            onward[i - 1].start()

    offsets_across.wait()
    offsets_onward.start()
    to_across[PIECES - 1].wait()
    onward[PIECES - 1].start()
    for copy in [offsets_onward] + onward:
        copy.wait()
    spread_offsets(far)
    spread_offsets(beyond)
    limit = count[...]
    for i in range(PATCHES // CHUNK):
        at = slice(i * CHUNK, (i + 1) * CHUNK)
        peak, grown, total = score(i, far, beyond)
        near_peak, near_total = near[i]
        top = jnp.maximum(peak, near_peak)
        lift, near_lift = jnp.exp(peak - top), jnp.exp(near_peak - top)
        where = lax.broadcasted_iota(jnp.int32, (1, CHUNK), 1) + i * CHUNK
        scale = jnp.where(where < limit, 1.0 / (total * lift + near_total * near_lift), 0.0)
        for k, weight in ((0, mass[:, at] * (scale * near_lift)), (1, grown * (scale * lift))):
            rows = slice(k * 512, (k + 1) * 512)
            weight = weight.astype(BF16)
            gamma[rows, at] = weight
            weight = weight.astype(F32)
            part = weight[:, :128]
            for m in range(1, CHUNK // 128):
                part = part + weight[:, m * 128 : m * 128 + 128]
            if i == 0:
                zeroth[rows] = part
            else:
                zeroth[rows] += part

    pl.semaphore_wait(heard.at[1], 3)

    tally = jnp.broadcast_to(limit.astype(F32), (1, 128))
    for h, order in ((0, 0), (1, 2)):
        for half in range(2):
            for ref, place in ((sums_held, order), (sums_give, order + 1)):
                start = place * BLOCK + half * 128
                ref[h, half, 0] = jnp.sum(zeroth[start : start + 128].T, axis=0, keepdims=True)
                ref[h, half, 1] = tally
    sums_copy = remote(sums_give, sums_take, sums_pair.at[0], sums_pair.at[1], partner)
    sums_copy.start()

    def statistics(place):
        stats = jnp.dot(gamma[place * BLOCK : (place + 1) * BLOCK, :], design[...], preferred_element_type=F32)
        return jnp.concatenate(
            [stats[:, :DIM].reshape(GROUP, 8, DIM), stats[:, DIM:].reshape(GROUP, 8, DIM)], axis=1
        )

    pair = []
    for k in range(2):
        give[k] = statistics(2 * k + 1).astype(BF16)
        pair.append(remote(give.at[k], take.at[k], pair_send.at[k], pair_recv.at[k], partner))
        pair[k].start()

    sums_copy.wait()
    sums_held[...] += sums_take[...]

    def scatter(k):
        def send(step, carry):
            step = 2 * step + k
            to = lax.rem(me + step, CHIPS)
            remote(held.at[k, to // 2], landed.at[CHIPS - step], scatter_send, scatter_recv, chip(to)).start()
            return carry

        lax.fori_loop(1 - k, GROUP, send, 0)

    owner = row * 4 + col
    adds = lax.rem(owner, 16) == 5
    lines_out = []
    for h, block in ((0, comp), (1, far)):
        for half in range(2):
            to = (4 * half + 1) * 8 + 2 + block // 2
            lines_out.append((to, remote(
                sums_held.at[h, half], sums_landed.at[lax.rem(me - to + CHIPS, CHIPS)],
                sums_send, sums_recv, (4 * half + 1, 1, block),
            )))
            @pl.when(to != me)
            def _():
                lines_out[-1][1].start()

    for k in range(2):
        mine = statistics(2 * k)
        pair[k].wait()
        held[k] = (mine + take[k].astype(F32)).astype(BF16)
        scatter(k)

    landed[0] = held[0, owner]

    def pass_on(step, carry):
        to = owner // 16 * 16 + lax.rem(lax.rem(owner, 16) + step, 16)
        remote(
            sums_total, sums_total, total_send, total_recv, (to // 4, lax.rem(to, 4), comp)
        ).start()
        return carry

    @pl.when(adds)
    def _():
        arrived = sums_landed.at[pl.ds(1, CHIPS - 1)]
        sums_landed[0] = sums_held[0, owner // 16]
        remote(arrived, arrived, sums_send, sums_recv, partner).wait_recv()
        sums_total[...] = jnp.sum(sums_landed[...], axis=0)
        lax.fori_loop(1, 16, pass_on, 0)

    for to, copy in lines_out:
        @pl.when(to != me)
        def _():
            copy.wait_send()

    rows = pl.ds(pl.multiple_of(owner * 8, 8), 8)
    centre = means[rows, :]
    inverse = precisions[rows, :]
    root = jnp.sqrt(inverse)
    share = jnp.exp(own_logs[rows, :1])
    all_but_own = landed.at[pl.ds(1, CHIPS - 1)]
    everyone = remote(all_but_own, all_but_own, scatter_send, scatter_recv, partner)
    everyone.wait_send()
    everyone.wait_recv()
    total = jnp.sum(landed[...].astype(F32), axis=0)

    @pl.when(adds)
    def _():
        sent = sums_landed.at[pl.ds(0, 15)]
        remote(sent, sent, total_send, total_recv, partner).wait_send()

    @pl.when(jnp.logical_not(adds))
    def _():
        remote(sums_total, sums_total, total_send, total_recv, partner).wait_recv()

    sums = sums_total[...]
    sums_column[...] = column(sums[0])
    patches = sums[1][:, :1]
    first = total[:8]
    second = total[8:]
    amount = sums_column[pl.ds(pl.multiple_of(lax.rem(owner, 16) * 8, 8), 8), :]
    amount = jnp.concatenate([amount, amount], axis=1)
    mean_fisher = (first - centre * amount) * root / jnp.sqrt(patches * share)
    var_fisher = (
        second * inverse - 2.0 * centre * inverse * first + (centre * centre * inverse - 1.0) * amount
    ) / jnp.sqrt(2.0 * patches * share)
    gathered[owner] = jnp.concatenate([mean_fisher, var_fisher], axis=0).astype(BF16)

    def gather(step, carry):
        to = lax.rem(owner + step, GROUP)
        remote(
            gathered.at[owner], gathered.at[owner], gather_send, gather_recv, (to // 4, lax.rem(to, 4), comp)
        ).start()
        return carry

    lax.fori_loop(1, GROUP, gather, 0)
    others = remote(gathered.at[pl.ds(1, GROUP - 1)], gathered.at[pl.ds(1, GROUP - 1)], gather_send, gather_recv, partner)
    others.wait_send()
    others.wait_recv()
    out[...] = gathered[...]


def shards(features, conv_weight, conv_bias, means, precisions, mix_logits, tissue_counts):
    vmem = pl.BlockSpec(memory_space=pltpu.VMEM)
    hbm = pl.BlockSpec(memory_space=pltpu.HBM)
    dma = pltpu.SemaphoreType.DMA
    fisher = pl.pallas_call(
        kernel,
        out_shape=pltpu.VMEM((GROUP, 16, DIM), BF16),
        in_specs=[hbm] * 7,
        out_specs=vmem,
        scratch_shapes=[
            pltpu.VMEM((HEIGHT + 2, WIDTH, CHAN), BF16),
            pltpu.VMEM((3, 3, CHAN, DIM), BF16),
            pltpu.VMEM((1, DIM), F32),
            pltpu.VMEM((8, 1, 128), F32),
            pltpu.VMEM((1, 1), jnp.int32),
            pltpu.VMEM((BLOCK, DIM), F32),
            pltpu.VMEM((BLOCK, DIM), F32),
            pltpu.VMEM((2, WIDTH, CHAN), BF16),
            pltpu.VMEM((HEIGHT, WIDTH, DIM), F32),
            pltpu.VMEM((2, HEIGHT, CHAN), BF16),
            pltpu.VMEM((2, 2, 16, 128), BF16),
            pltpu.VMEM((2, 2, 16, 128), BF16),
            pltpu.VMEM((2, HEIGHT, CHAN), BF16),
            pltpu.VMEM((4, BLOCK, 2 * DIM), BF16),
            pltpu.VMEM((4, 2, 8, 128), F32),
            pltpu.VMEM((4, BLOCK, 128), F32),
            pltpu.VMEM((BLOCK, 128), F32),
            pltpu.VMEM((PATCHES, 2 * DIM), BF16),
            pltpu.VMEM((COMPS // 2, PATCHES), F32),
            pltpu.VMEM((COMPS, PATCHES), BF16),
            pltpu.VMEM((COMPS, 128), F32),
            pltpu.VMEM((2, GROUP, 16, DIM), BF16),
            pltpu.VMEM((2, GROUP, 16, DIM), BF16),
            pltpu.VMEM((2, GROUP, 16, DIM), BF16),
            pltpu.VMEM((CHIPS, 16, DIM), BF16),
            pltpu.VMEM((GROUP, 16, DIM), BF16),
            pltpu.VMEM((2, 2, 2, 1, 128), F32),
            pltpu.VMEM((2, 2, 2, 1, 128), F32),
            pltpu.VMEM((2, 2, 2, 1, 128), F32),
            pltpu.VMEM((CHIPS, 2, 1, 128), F32),
            pltpu.VMEM((2, 1, 128), F32),
            pltpu.VMEM((128, 128), F32),
            dma((7,)), dma((8,)), dma((8,)), dma((3, PIECES + 1)), dma((3, PIECES + 1)), dma((2,)), dma((2,)),
            dma((2,)), dma, dma, dma, dma, dma, dma, dma, dma, pltpu.SemaphoreType.REGULAR((2,)),
        ],
        compiler_params=pltpu.CompilerParams(
            collective_id=0, has_side_effects=True, vmem_limit_bytes=56 * 2**20
        ),
    )(
        features, conv_weight, conv_bias.reshape(1, DIM), means, precisions,
        mix_logits.reshape(8, 1, 128), tissue_counts,
    )
    return tuple(
        fisher[:, 8 * k : 8 * k + 8].astype(F32).reshape(BLOCK, DIM) for k in range(2)
    )


def solution(mesh):
    in_specs = (
        P("row", ("col", "comp"), None),
        P(),
        P(),
        P("comp", None),
        P("comp", None),
        P(),
        P("row", ("col", "comp")),
    )
    out_specs = (P("comp", None), P("comp", None))
    return jax.shard_map(shards, mesh=mesh, in_specs=in_specs, out_specs=out_specs, check_vma=False)
```

```python
import functools

import jax
import jax.numpy as jnp
from jax import lax
from jax.experimental import pallas as pl
from jax.experimental.pallas import tpu as pltpu
from jax.sharding import PartitionSpec as P

F32 = jnp.float32
BF16 = jnp.bfloat16
MESH = pl.DeviceIdType.MESH

HEIGHT, WIDTH, CHAN, DIM = 32, 64, 512, 256
COMPS, BLOCK = 1024, 256
PATCHES = HEIGHT * WIDTH
CHUNK = 512
ROWS = CHUNK // WIDTH
CHIPS = 64
GROUP = 32
PIECES = 4


def signal(sem, device):
    pl.semaphore_signal(sem, inc=1, device_id=device, device_id_type=MESH)


def remote(src, dst, send_sem, recv_sem, device):
    return pltpu.make_async_remote_copy(
        src_ref=src, dst_ref=dst, send_sem=send_sem, recv_sem=recv_sem,
        device_id=device, device_id_type=MESH,
    )


def column(line):
    return jnp.broadcast_to(line, (128, 128)).T


def kernel(
    features, conv_weight, bias_in, means_in, precisions_in, logits_in, count_in, out,
    x, w, bias, logits, count, means, precisions, ends, raw, sides, corners, corners_out, edge, panel, offset_lines, offsets,
    own_logs, design, mass, gamma, zeroth, give, take, held, landed, gathered,
    sums_give, sums_take, sums_held, sums_landed, sums_total, sums_column,
    load_sem, halo_send, halo_recv, panel_send, panel_recv, pair_send, pair_recv,
    sums_pair, scatter_send, scatter_recv, sums_send, sums_recv, gather_send, gather_recv, total_send, total_recv, heard,
):
    row, col, comp = lax.axis_index("row"), lax.axis_index("col"), lax.axis_index("comp")
    core = lax.rem(comp, 2)
    upper = comp // 2
    tile = col * 4 + comp
    me = row * 8 + col * 2 + upper
    partner = (row, col, comp + 1 - 2 * core)
    across = (row + 1 - 2 * lax.rem(row, 2), col, lax.rem(comp + 2, 4))

    def chip(number):
        return (number // 8, lax.rem(number // 2, 4), 2 * lax.rem(number, 2) + core)

    def spot(down, right):
        there = tile + right
        return (row + down, there // 4, lax.rem(there, 4))

    def exists(down, right):
        ok = jnp.bool_(True)
        if down < 0:
            ok = row > 0
        if down > 0:
            ok = row < 7
        if right < 0:
            ok = jnp.logical_and(ok, tile > 0)
        if right > 0:
            ok = jnp.logical_and(ok, tile < 15)
        return ok

    loads = [
        pltpu.make_async_copy(src, dst, load_sem.at[k])
        for k, (src, dst) in enumerate((
            (means_in, means), (precisions_in, precisions), (features, x.at[pl.ds(1, HEIGHT)]), (logits_in, logits),
            (bias_in, bias), (count_in, count), (conv_weight, w),
        ))
    ]
    for load in loads[:6]:
        load.start()

    barrier = pltpu.get_barrier_semaphore()
    lower = lax.rem(row, 2)
    z_peers = [(row, lax.rem(col + k, 4), comp) for k in (1, 2, 3)]
    x_peers = [(lax.rem(row + 2 * k, 8), col, comp) for k in (1, 2, 3)]
    y_peers = [
        (row + 1 - 2 * lower, col, comp),
        (row, col, lax.rem(comp + 2, 4)),
        across,
    ]
    around = [(-1, 0), (1, 0), (0, -1), (0, 1), (-1, -1), (-1, 1), (1, -1), (1, 1)]
    for device in y_peers + [partner] + x_peers + z_peers:
        signal(barrier, device)
    greeted = 10
    for place in around:
        @pl.when(exists(*place))
        def _():
            signal(barrier, spot(*place))
        greeted = greeted + exists(*place).astype(jnp.int32)

    loads[0].wait()
    loads[1].wait()
    centres = means[...]
    inverse = precisions[...]
    panel[comp] = jnp.concatenate(
        [(centres * inverse).astype(BF16), (-0.5 * inverse).astype(BF16)], axis=1
    )
    pl.semaphore_wait(barrier, greeted)

    def hear(peers, k):
        for device in peers:
            signal(heard.at[k], device)

    far = lax.rem(comp + 2, 4)
    beyond = far + 1 - 2 * core

    def panel_copy(block, piece, slot, device):
        rows = panel.at[block, pl.ds(piece * (BLOCK // PIECES), BLOCK // PIECES)]
        return remote(rows, rows, panel_send.at[slot, piece], panel_recv.at[slot, piece], device)

    def offset_copy(block, slot, device):
        lines = offset_lines.at[block]
        return remote(lines, lines, panel_send.at[slot, PIECES], panel_recv.at[slot, PIECES], device)

    to_across = [panel_copy(comp, piece, 0, across) for piece in range(PIECES)]
    to_partner = [panel_copy(comp, piece, 1, partner) for piece in range(PIECES)]
    onward = [panel_copy(far, piece, 2, partner) for piece in range(PIECES)]
    offsets_across, offsets_partner, offsets_onward = (
        offset_copy(comp, 0, across), offset_copy(comp, 1, partner), offset_copy(far, 2, partner)
    )

    loads[2].wait()
    loads[6].start()
    halos = []

    def halo(index, down, right, src, dst):
        halos.append((index, down, right, remote(src, dst, halo_send.at[index], halo_recv.at[index], spot(down, right))))
        @pl.when(exists(down, right))
        def _():
            halos[-1][3].start()

    halo(0, -1, 0, x.at[1], ends.at[1])
    halo(1, 1, 0, x.at[HEIGHT], ends.at[0])
    flat = x[1 : HEIGHT + 1].reshape(PATCHES, CHAN)
    line = lax.broadcasted_iota(jnp.int32, (2 * HEIGHT, PATCHES), 0)
    patch = lax.broadcasted_iota(jnp.int32, (2 * HEIGHT, PATCHES), 1)
    wanted = jnp.where(line < HEIGHT, line * WIDTH, (line - HEIGHT) * WIDTH + WIDTH - 1)
    picked = jnp.dot(
        jnp.where(patch == wanted, 1.0, 0.0).astype(BF16), flat, preferred_element_type=F32
    ).astype(BF16)
    edge[0] = picked[:HEIGHT]
    edge[1] = picked[HEIGHT:]
    halo(6, 0, -1, edge.at[0], sides.at[1])
    halo(7, 0, 1, edge.at[1], sides.at[0])
    for index, down, right in ((2, -1, -1), (3, -1, 1), (4, 1, -1), (5, 1, 1)):
        side, end = (1 - right) // 2, (1 - down) // 2
        k = 0 if down < 0 else HEIGHT - 1
        spread = picked[(1 - side) * HEIGHT + k : (1 - side) * HEIGHT + k + 1].astype(F32)
        spread = jnp.concatenate(
            [spread[:, 128 * q : 128 * q + 128] for q in range(4)] + [jnp.zeros((12, 128), F32)], axis=0
        )
        corners_out[side, end] = spread.astype(BF16)
        halo(index, down, right, corners_out.at[side, end], corners.at[side, end])

    for copy in to_across + to_partner:
        copy.start()
    hear(x_peers, 0)

    loads[3].wait()
    lines = logits[...]
    top = jnp.max(jnp.max(lines, axis=0), axis=1, keepdims=True)
    norm = top + jnp.log(jnp.sum(jnp.sum(jnp.exp(lines - top[None]), axis=0), axis=1, keepdims=True))
    logs = jnp.concatenate([column(logits[2 * comp] - norm), column(logits[2 * comp + 1] - norm)], axis=0)
    own_logs[...] = logs
    constant = 0.5 * jnp.sum(jnp.log(inverse), axis=1, keepdims=True) - 0.5 * jnp.sum(
        inverse * centres * centres, axis=1, keepdims=True
    )
    own_offset = logs + constant
    for half in range(2):
        offset_lines[comp, half] = own_offset[half * 128 : half * 128 + 128].T[:8]
    offsets_across.start()
    offsets_partner.start()

    x[0] = jnp.zeros((WIDTH, CHAN), BF16)
    x[HEIGHT + 1] = jnp.zeros((WIDTH, CHAN), BF16)

    @pl.when(row == 0)
    def _():
        ends[0] = jnp.zeros((WIDTH, CHAN), BF16)

    @pl.when(row == 7)
    def _():
        ends[1] = jnp.zeros((WIDTH, CHAN), BF16)

    for side, edge_tile in ((0, 0), (1, 15)):
        @pl.when(tile == edge_tile)
        def _():
            sides[side] = jnp.zeros((HEIGHT, CHAN), BF16)

        for end, edge_row in ((0, 0), (1, 7)):
            @pl.when(jnp.logical_or(tile == edge_tile, row == edge_row))
            def _():
                corners[side, end] = jnp.zeros((16, 128), BF16)

    for load in loads[4:]:
        load.wait()

    def shifted(y, height):
        c = lax.broadcasted_iota(jnp.int32, (height, WIDTH, DIM), 1)
        count = height * WIDTH
        before = jnp.where(c == 0, 0.0, pltpu.roll(y[0], 1, 0).reshape(height, WIDTH, DIM))
        after = jnp.where(c == WIDTH - 1, 0.0, pltpu.roll(y[2], count - 1, 0).reshape(height, WIDTH, DIM))
        return y[1].reshape(height, WIDTH, DIM) + before + after

    def convolve(i):
        lhs = jnp.concatenate(
            [x[i * ROWS + k : i * ROWS + k + ROWS].reshape(CHUNK, CHAN) for k in range(3)], axis=1
        )
        y = [
            jnp.dot(lhs, w[:, tap].reshape(3 * CHAN, DIM), preferred_element_type=F32)
            for tap in range(3)
        ]
        raw[i * ROWS : (i + 1) * ROWS] = shifted(y, ROWS) + bias[...].reshape(1, 1, DIM)

    for i in range(PATCHES // CHUNK):
        convolve(i)

    pl.semaphore_wait(heard.at[0], 3)
    hear(y_peers, 1)
    for index, down, right, copy in halos:
        @pl.when(exists(down, right))
        def _():
            copy.wait_send()

        @pl.when(exists(-down, -right))
        def _():
            copy.wait_recv()

    def corner(side, end):
        tile_of = corners[side, end].astype(F32)
        line = jnp.concatenate([tile_of[q : q + 1] for q in range(4)], axis=1)
        return jnp.broadcast_to(line, (16, CHAN)).astype(BF16)

    beside = [jnp.concatenate([sides[side], corner(side, 0), corner(side, 1)], axis=0) for side in range(2)]
    products = {}
    for k in range(3):
        for tap in range(3):
            lhs = []
            if k != 1:
                lhs.append(ends[k // 2])
            if tap != 1:
                lhs.append(beside[tap // 2])
            if lhs:
                products[k, tap] = jnp.dot(
                    lhs[0] if len(lhs) == 1 else jnp.concatenate(lhs, axis=0), w[k, tap], preferred_element_type=F32
                )
    for k, at in ((0, 0), (2, HEIGHT - 1)):
        raw[at] += shifted([products[k, tap][:WIDTH] for tap in range(3)], 1)[0]
    r = lax.broadcasted_iota(jnp.int32, (HEIGHT, DIM), 0)
    c = lax.broadcasted_iota(jnp.int32, (HEIGHT, 8, DIM), 1)
    for side, tap in ((0, 0), (1, 2)):
        y = [products[k, tap][-WIDTH:] for k in range(3)]
        above = jnp.where(r == 0, y[0][32:33], pltpu.roll(y[0][:HEIGHT], 1, 0))
        below = jnp.where(r == HEIGHT - 1, y[2][48:49], pltpu.roll(y[2][:HEIGHT], HEIGHT - 1, 0))
        more = (above + y[1][:HEIGHT] + below).reshape(HEIGHT, 1, DIM)
        if side == 0:
            raw[:, :8] += jnp.where(c == 0, more, 0.0)
        else:
            raw[:, WIDTH - 8 :] += jnp.where(c == 7, more, 0.0)

    for i in range(PATCHES // CHUNK):
        encoded = raw[i * ROWS : (i + 1) * ROWS].reshape(CHUNK, DIM).astype(BF16)
        wide = encoded.astype(F32)
        design[i * CHUNK : (i + 1) * CHUNK, :DIM] = encoded
        design[i * CHUNK : (i + 1) * CHUNK, DIM:] = (wide * wide).astype(BF16)

    for copy in to_partner + [offsets_partner]:
        copy.wait()

    def score(i, first, second):
        flipped = design[i * CHUNK : (i + 1) * CHUNK, :DIM].T
        wide = flipped.astype(F32)
        rhs = jnp.concatenate([flipped, (wide * wide).astype(BF16)], axis=0)
        lhs = jnp.concatenate([panel[first], panel[second]], axis=0)
        add = jnp.concatenate([offsets[first], offsets[second]], axis=0)
        scores = jnp.dot(lhs, rhs, preferred_element_type=F32) + jnp.concatenate([add] * (CHUNK // 128), axis=1)
        peak = jnp.max(scores, axis=0, keepdims=True)
        grown = jnp.exp(scores - peak)
        return peak, grown, jnp.sum(grown, axis=0, keepdims=True)

    def spread_offsets(block):
        for half in range(2):
            offsets[block, half * 128 : half * 128 + 128] = column(offset_lines[block, half, :1])

    spread_offsets(comp)
    spread_offsets(comp + 1 - 2 * core)
    near = []
    for i in range(PATCHES // CHUNK):
        peak, grown, total = score(i, comp, comp + 1 - 2 * core)
        mass[:, i * CHUNK : (i + 1) * CHUNK] = grown
        near.append((peak, total))
        if i >= 1:
            to_across[i - 1].wait()
            onward[i - 1].start()

    offsets_across.wait()
    offsets_onward.start()
    to_across[PIECES - 1].wait()
    onward[PIECES - 1].start()
    for copy in [offsets_onward] + onward:
        copy.wait()
    spread_offsets(far)
    spread_offsets(beyond)
    pl.semaphore_wait(heard.at[1], 3)
    limit = count[...]
    for i in range(PATCHES // CHUNK):
        at = slice(i * CHUNK, (i + 1) * CHUNK)
        peak, grown, total = score(i, far, beyond)
        near_peak, near_total = near[i]
        top = jnp.maximum(peak, near_peak)
        lift, near_lift = jnp.exp(peak - top), jnp.exp(near_peak - top)
        where = lax.broadcasted_iota(jnp.int32, (1, CHUNK), 1) + i * CHUNK
        scale = jnp.where(where < limit, 1.0 / (total * lift + near_total * near_lift), 0.0)
        for k, weight in ((0, mass[:, at] * (scale * near_lift)), (1, grown * (scale * lift))):
            rows = slice(k * 512, (k + 1) * 512)
            weight = weight.astype(BF16)
            gamma[rows, at] = weight
            weight = weight.astype(F32)
            part = weight[:, :128]
            for m in range(1, CHUNK // 128):
                part = part + weight[:, m * 128 : m * 128 + 128]
            if i == 0:
                zeroth[rows] = part
            else:
                zeroth[rows] += part

    tally = jnp.broadcast_to(limit.astype(F32), (1, 128))
    for h, order in ((0, 0), (1, 2)):
        for half in range(2):
            for ref, place in ((sums_held, order), (sums_give, order + 1)):
                start = place * BLOCK + half * 128
                ref[h, half, 0] = jnp.sum(zeroth[start : start + 128].T, axis=0, keepdims=True)
                ref[h, half, 1] = tally
    sums_copy = remote(sums_give, sums_take, sums_pair.at[0], sums_pair.at[1], partner)

    def statistics(place):
        stats = jnp.dot(gamma[place * BLOCK : (place + 1) * BLOCK, :], design[...], preferred_element_type=F32)
        return jnp.concatenate(
            [stats[:, :DIM].reshape(GROUP, 8, DIM), stats[:, DIM:].reshape(GROUP, 8, DIM)], axis=1
        )

    pair = []
    for k in range(2):
        pair.append(remote(give.at[k], take.at[k], pair_send.at[k], pair_recv.at[k], partner))
    for k in (1, 0):
        give[k] = statistics(2 * k + 1).astype(BF16)
        pair[k].start()
        if k == 1:
            sums_copy.start()

    sums_copy.wait()
    sums_held[...] += sums_take[...]

    def apart(number):
        return [number, number + 1 - 2 * lax.rem(number, 2), lax.rem(number + 2, 4), 3 - number]

    x_apart, z_apart = apart(row // 2), apart(col)
    y_apart = [lower, 1 - lower]

    def owners(k):
        hops = [0, 1, 2, 1]
        places = [(dx, dy, dz) for dx in range(4) for dy in range(2) for dz in range(4)]
        places = [p for p in places if k or any(p)]
        return sorted(places, key=lambda p: -(hops[p[0]] + hops[p[1] + 2 * k] + hops[p[2]]))

    def scatter(k):
        for dx, dy, dz in owners(k):
            to_row, to_col = 2 * x_apart[dx] + y_apart[dy], z_apart[dz]
            remote(
                held.at[k, to_row * 4 + to_col], landed.at[k * GROUP + dx * 8 + dy * 4 + dz],
                scatter_send, scatter_recv, (to_row, to_col, far if k else comp),
            ).start()

    owner = row * 4 + col
    adds = lax.rem(owner, 16) == 5
    lines_out = []
    for h, block in ((0, comp), (1, far)):
        for half in range(2):
            to = (4 * half + 1) * 8 + 2 + block // 2
            lines_out.append((to, remote(
                sums_held.at[h, half], sums_landed.at[lax.rem(me - to + CHIPS, CHIPS)],
                sums_send, sums_recv, (4 * half + 1, 1, block),
            )))
            @pl.when(to != me)
            def _():
                lines_out[-1][1].start()

    for k in (1, 0):
        mine = statistics(2 * k)
        pair[k].wait()
        held[k] = (mine + take[k].astype(F32)).astype(BF16)
        scatter(k)

    landed[0] = held[0, owner]

    def pass_on(step, carry):
        to = owner // 16 * 16 + lax.rem(lax.rem(owner, 16) + step, 16)
        remote(
            sums_total, sums_total, total_send, total_recv, (to // 4, lax.rem(to, 4), comp)
        ).start()
        return carry

    @pl.when(adds)
    def _():
        arrived = sums_landed.at[pl.ds(1, CHIPS - 1)]
        sums_landed[0] = sums_held[0, owner // 16]
        remote(arrived, arrived, sums_send, sums_recv, partner).wait_recv()
        sums_total[...] = jnp.sum(sums_landed[...], axis=0)
        lax.fori_loop(1, 16, pass_on, 0)

    for to, copy in lines_out:
        @pl.when(to != me)
        def _():
            copy.wait_send()

    rows = pl.ds(pl.multiple_of(owner * 8, 8), 8)
    centre = means[rows, :]
    inverse = precisions[rows, :]
    root = jnp.sqrt(inverse)
    share = jnp.exp(own_logs[rows, :1])
    all_but_own = landed.at[pl.ds(1, CHIPS - 1)]
    everyone = remote(all_but_own, all_but_own, scatter_send, scatter_recv, partner)
    everyone.wait_send()
    everyone.wait_recv()
    total = jnp.sum(landed[...].astype(F32), axis=0)

    @pl.when(adds)
    def _():
        sent = sums_landed.at[pl.ds(0, 15)]
        remote(sent, sent, total_send, total_recv, partner).wait_send()

    @pl.when(jnp.logical_not(adds))
    def _():
        remote(sums_total, sums_total, total_send, total_recv, partner).wait_recv()

    sums = sums_total[...]
    sums_column[...] = column(sums[0])
    patches = sums[1][:, :1]
    first = total[:8]
    second = total[8:]
    amount = sums_column[pl.ds(pl.multiple_of(lax.rem(owner, 16) * 8, 8), 8), :]
    amount = jnp.concatenate([amount, amount], axis=1)
    mean_fisher = (first - centre * amount) * root / jnp.sqrt(patches * share)
    var_fisher = (
        second * inverse - 2.0 * centre * inverse * first + (centre * centre * inverse - 1.0) * amount
    ) / jnp.sqrt(2.0 * patches * share)
    gathered[owner] = jnp.concatenate([mean_fisher, var_fisher], axis=0).astype(BF16)

    for dx, dy, dz in owners(0):
        remote(
            gathered.at[owner], gathered.at[owner], gather_send, gather_recv,
            (2 * x_apart[dx] + y_apart[dy], z_apart[dz], comp),
        ).start()
    others = remote(gathered.at[pl.ds(1, GROUP - 1)], gathered.at[pl.ds(1, GROUP - 1)], gather_send, gather_recv, partner)
    others.wait_send()
    others.wait_recv()
    out[...] = gathered[...]


def shards(features, conv_weight, conv_bias, means, precisions, mix_logits, tissue_counts):
    vmem = pl.BlockSpec(memory_space=pltpu.VMEM)
    hbm = pl.BlockSpec(memory_space=pltpu.HBM)
    dma = pltpu.SemaphoreType.DMA
    fisher = pl.pallas_call(
        kernel,
        out_shape=pltpu.VMEM((GROUP, 16, DIM), BF16),
        in_specs=[hbm] * 7,
        out_specs=vmem,
        scratch_shapes=[
            pltpu.VMEM((HEIGHT + 2, WIDTH, CHAN), BF16),
            pltpu.VMEM((3, 3, CHAN, DIM), BF16),
            pltpu.VMEM((1, DIM), F32),
            pltpu.VMEM((8, 1, 128), F32),
            pltpu.VMEM((1, 1), jnp.int32),
            pltpu.VMEM((BLOCK, DIM), F32),
            pltpu.VMEM((BLOCK, DIM), F32),
            pltpu.VMEM((2, WIDTH, CHAN), BF16),
            pltpu.VMEM((HEIGHT, WIDTH, DIM), F32),
            pltpu.VMEM((2, HEIGHT, CHAN), BF16),
            pltpu.VMEM((2, 2, 16, 128), BF16),
            pltpu.VMEM((2, 2, 16, 128), BF16),
            pltpu.VMEM((2, HEIGHT, CHAN), BF16),
            pltpu.VMEM((4, BLOCK, 2 * DIM), BF16),
            pltpu.VMEM((4, 2, 8, 128), F32),
            pltpu.VMEM((4, BLOCK, 128), F32),
            pltpu.VMEM((BLOCK, 128), F32),
            pltpu.VMEM((PATCHES, 2 * DIM), BF16),
            pltpu.VMEM((COMPS // 2, PATCHES), F32),
            pltpu.VMEM((COMPS, PATCHES), BF16),
            pltpu.VMEM((COMPS, 128), F32),
            pltpu.VMEM((2, GROUP, 16, DIM), BF16),
            pltpu.VMEM((2, GROUP, 16, DIM), BF16),
            pltpu.VMEM((2, GROUP, 16, DIM), BF16),
            pltpu.VMEM((CHIPS, 16, DIM), BF16),
            pltpu.VMEM((GROUP, 16, DIM), BF16),
            pltpu.VMEM((2, 2, 2, 1, 128), F32),
            pltpu.VMEM((2, 2, 2, 1, 128), F32),
            pltpu.VMEM((2, 2, 2, 1, 128), F32),
            pltpu.VMEM((CHIPS, 2, 1, 128), F32),
            pltpu.VMEM((2, 1, 128), F32),
            pltpu.VMEM((128, 128), F32),
            dma((7,)), dma((8,)), dma((8,)), dma((3, PIECES + 1)), dma((3, PIECES + 1)), dma((2,)), dma((2,)),
            dma((2,)), dma, dma, dma, dma, dma, dma, dma, dma, pltpu.SemaphoreType.REGULAR((2,)),
        ],
        compiler_params=pltpu.CompilerParams(
            collective_id=0, has_side_effects=True, vmem_limit_bytes=56 * 2**20
        ),
    )(
        features, conv_weight, conv_bias.reshape(1, DIM), means, precisions,
        mix_logits.reshape(8, 1, 128), tissue_counts,
    )
    return tuple(
        fisher[:, 8 * k : 8 * k + 8].astype(F32).reshape(BLOCK, DIM) for k in range(2)
    )


def solution(mesh):
    in_specs = (
        P("row", ("col", "comp"), None),
        P(),
        P(),
        P("comp", None),
        P("comp", None),
        P(),
        P("row", ("col", "comp")),
    )
    out_specs = (P("comp", None), P("comp", None))
    return jax.shard_map(shards, mesh=mesh, in_specs=in_specs, out_specs=out_specs, check_vma=False)
```

```python
import functools

import jax
import jax.numpy as jnp
from jax import lax
from jax.experimental import pallas as pl
from jax.experimental.pallas import tpu as pltpu
from jax.sharding import PartitionSpec as P

F32 = jnp.float32
BF16 = jnp.bfloat16
MESH = pl.DeviceIdType.MESH

HEIGHT, WIDTH, CHAN, DIM = 32, 64, 512, 256
COMPS, BLOCK = 1024, 256
PATCHES = HEIGHT * WIDTH
CHUNK = 512
ROWS = CHUNK // WIDTH
CHIPS = 64
GROUP = 32
PIECES = 4


def signal(sem, device):
    pl.semaphore_signal(sem, inc=1, device_id=device, device_id_type=MESH)


def remote(src, dst, send_sem, recv_sem, device):
    return pltpu.make_async_remote_copy(
        src_ref=src, dst_ref=dst, send_sem=send_sem, recv_sem=recv_sem,
        device_id=device, device_id_type=MESH,
    )


def column(line):
    return jnp.broadcast_to(line, (128, 128)).T


def kernel(
    features, conv_weight, bias_in, means_in, precisions_in, logits_in, count_in, out,
    x, w, bias, logits, count, means, precisions, ends, raw, sides, corners, corners_out, edge, panel, offset_lines, offsets,
    own_logs, design, mass, gamma, zeroth, give, take, held, landed, gathered,
    sums_give, sums_take, sums_held, sums_landed, sums_total, sums_column,
    load_sem, halo_send, halo_recv, panel_send, panel_recv, pair_send, pair_recv,
    sums_pair, scatter_send, scatter_recv, sums_send, sums_recv, gather_send, gather_recv, total_send, total_recv, heard,
):
    row, col, comp = lax.axis_index("row"), lax.axis_index("col"), lax.axis_index("comp")
    core = lax.rem(comp, 2)
    upper = comp // 2
    tile = col * 4 + comp
    me = row * 8 + col * 2 + upper
    partner = (row, col, comp + 1 - 2 * core)
    across = (row + 1 - 2 * lax.rem(row, 2), col, lax.rem(comp + 2, 4))

    def chip(number):
        return (number // 8, lax.rem(number // 2, 4), 2 * lax.rem(number, 2) + core)

    def spot(down, right):
        there = tile + right
        return (row + down, there // 4, lax.rem(there, 4))

    def exists(down, right):
        ok = jnp.bool_(True)
        if down < 0:
            ok = row > 0
        if down > 0:
            ok = row < 7
        if right < 0:
            ok = jnp.logical_and(ok, tile > 0)
        if right > 0:
            ok = jnp.logical_and(ok, tile < 15)
        return ok

    loads = [
        pltpu.make_async_copy(src, dst, load_sem.at[k])
        for k, (src, dst) in enumerate((
            (means_in, means), (precisions_in, precisions), (features, x.at[pl.ds(1, HEIGHT)]), (logits_in, logits),
            (bias_in, bias), (count_in, count), (conv_weight, w),
        ))
    ]
    for load in loads[:6]:
        load.start()

    barrier = pltpu.get_barrier_semaphore()
    lower = lax.rem(row, 2)
    z_peers = [(row, lax.rem(col + k, 4), comp) for k in (1, 2, 3)]
    x_peers = [(lax.rem(row + 2 * k, 8), col, comp) for k in (1, 2, 3)]
    y_peers = [
        (row + 1 - 2 * lower, col, comp),
        (row, col, lax.rem(comp + 2, 4)),
        across,
    ]
    around = [(-1, 0), (1, 0), (0, -1), (0, 1), (-1, -1), (-1, 1), (1, -1), (1, 1)]
    for device in y_peers + [partner] + x_peers + z_peers:
        signal(barrier, device)
    greeted = 10
    for place in around:
        @pl.when(exists(*place))
        def _():
            signal(barrier, spot(*place))
        greeted = greeted + exists(*place).astype(jnp.int32)

    loads[0].wait()
    loads[1].wait()
    centres = means[...]
    inverse = precisions[...]
    panel[comp] = jnp.concatenate(
        [(centres * inverse).astype(BF16), (-0.5 * inverse).astype(BF16)], axis=1
    )
    pl.semaphore_wait(barrier, greeted)

    def hear(peers, k):
        for device in peers:
            signal(heard.at[k], device)

    far = lax.rem(comp + 2, 4)
    beyond = far + 1 - 2 * core

    def panel_copy(block, piece, slot, device):
        rows = panel.at[block, pl.ds(piece * (BLOCK // PIECES), BLOCK // PIECES)]
        return remote(rows, rows, panel_send.at[slot, piece], panel_recv.at[slot, piece], device)

    def offset_copy(block, slot, device):
        lines = offset_lines.at[block]
        return remote(lines, lines, panel_send.at[slot, PIECES], panel_recv.at[slot, PIECES], device)

    to_across = [panel_copy(comp, piece, 0, across) for piece in range(PIECES)]
    to_partner = [panel_copy(comp, piece, 1, partner) for piece in range(PIECES)]
    onward = [panel_copy(far, piece, 2, partner) for piece in range(PIECES)]
    offsets_across, offsets_partner, offsets_onward = (
        offset_copy(comp, 0, across), offset_copy(comp, 1, partner), offset_copy(far, 2, partner)
    )

    loads[2].wait()
    loads[6].start()
    halos = []

    def halo(index, down, right, src, dst):
        halos.append((index, down, right, remote(src, dst, halo_send.at[index], halo_recv.at[index], spot(down, right))))
        @pl.when(exists(down, right))
        def _():
            halos[-1][3].start()

    halo(0, -1, 0, x.at[1], ends.at[1])
    halo(1, 1, 0, x.at[HEIGHT], ends.at[0])
    flat = x[1 : HEIGHT + 1].reshape(PATCHES, CHAN)
    line = lax.broadcasted_iota(jnp.int32, (2 * HEIGHT, PATCHES), 0)
    patch = lax.broadcasted_iota(jnp.int32, (2 * HEIGHT, PATCHES), 1)
    wanted = jnp.where(line < HEIGHT, line * WIDTH, (line - HEIGHT) * WIDTH + WIDTH - 1)
    picked = jnp.dot(
        jnp.where(patch == wanted, 1.0, 0.0).astype(BF16), flat, preferred_element_type=F32
    ).astype(BF16)
    edge[0] = picked[:HEIGHT]
    edge[1] = picked[HEIGHT:]
    halo(6, 0, -1, edge.at[0], sides.at[1])
    halo(7, 0, 1, edge.at[1], sides.at[0])
    for index, down, right in ((2, -1, -1), (3, -1, 1), (4, 1, -1), (5, 1, 1)):
        side, end = (1 - right) // 2, (1 - down) // 2
        k = 0 if down < 0 else HEIGHT - 1
        spread = picked[(1 - side) * HEIGHT + k : (1 - side) * HEIGHT + k + 1].astype(F32)
        spread = jnp.concatenate(
            [spread[:, 128 * q : 128 * q + 128] for q in range(4)] + [jnp.zeros((12, 128), F32)], axis=0
        )
        corners_out[side, end] = spread.astype(BF16)
        halo(index, down, right, corners_out.at[side, end], corners.at[side, end])

    for copy in to_across + to_partner:
        copy.start()
    hear(x_peers, 0)

    loads[3].wait()
    lines = logits[...]
    top = jnp.max(jnp.max(lines, axis=0), axis=1, keepdims=True)
    norm = top + jnp.log(jnp.sum(jnp.sum(jnp.exp(lines - top[None]), axis=0), axis=1, keepdims=True))
    logs = jnp.concatenate([column(logits[2 * comp] - norm), column(logits[2 * comp + 1] - norm)], axis=0)
    own_logs[...] = logs
    constant = 0.5 * jnp.sum(jnp.log(inverse), axis=1, keepdims=True) - 0.5 * jnp.sum(
        inverse * centres * centres, axis=1, keepdims=True
    )
    own_offset = logs + constant
    for half in range(2):
        offset_lines[comp, half] = own_offset[half * 128 : half * 128 + 128].T[:8]
    offsets_across.start()
    offsets_partner.start()

    x[0] = jnp.zeros((WIDTH, CHAN), BF16)
    x[HEIGHT + 1] = jnp.zeros((WIDTH, CHAN), BF16)

    @pl.when(row == 0)
    def _():
        ends[0] = jnp.zeros((WIDTH, CHAN), BF16)

    @pl.when(row == 7)
    def _():
        ends[1] = jnp.zeros((WIDTH, CHAN), BF16)

    for side, edge_tile in ((0, 0), (1, 15)):
        @pl.when(tile == edge_tile)
        def _():
            sides[side] = jnp.zeros((HEIGHT, CHAN), BF16)

        for end, edge_row in ((0, 0), (1, 7)):
            @pl.when(jnp.logical_or(tile == edge_tile, row == edge_row))
            def _():
                corners[side, end] = jnp.zeros((16, 128), BF16)

    for load in loads[4:]:
        load.wait()

    def shifted(y, height):
        c = lax.broadcasted_iota(jnp.int32, (height, WIDTH, DIM), 1)
        count = height * WIDTH
        before = jnp.where(c == 0, 0.0, pltpu.roll(y[0], 1, 0).reshape(height, WIDTH, DIM))
        after = jnp.where(c == WIDTH - 1, 0.0, pltpu.roll(y[2], count - 1, 0).reshape(height, WIDTH, DIM))
        return y[1].reshape(height, WIDTH, DIM) + before + after

    def convolve(i):
        lhs = jnp.concatenate(
            [x[i * ROWS + k : i * ROWS + k + ROWS].reshape(CHUNK, CHAN) for k in range(3)], axis=1
        )
        y = [
            jnp.dot(lhs, w[:, tap].reshape(3 * CHAN, DIM), preferred_element_type=F32)
            for tap in range(3)
        ]
        raw[i * ROWS : (i + 1) * ROWS] = shifted(y, ROWS) + bias[...].reshape(1, 1, DIM)

    for i in range(PATCHES // CHUNK):
        convolve(i)

    pl.semaphore_wait(heard.at[0], 3)
    hear(y_peers, 1)
    for index, down, right, copy in halos:
        @pl.when(exists(down, right))
        def _():
            copy.wait_send()

        @pl.when(exists(-down, -right))
        def _():
            copy.wait_recv()

    def corner(side, end):
        tile_of = corners[side, end].astype(F32)
        line = jnp.concatenate([tile_of[q : q + 1] for q in range(4)], axis=1)
        return jnp.broadcast_to(line, (16, CHAN)).astype(BF16)

    beside = [jnp.concatenate([sides[side], corner(side, 0), corner(side, 1)], axis=0) for side in range(2)]
    products = {}
    for k in range(3):
        for tap in range(3):
            lhs = []
            if k != 1:
                lhs.append(ends[k // 2])
            if tap != 1:
                lhs.append(beside[tap // 2])
            if lhs:
                products[k, tap] = jnp.dot(
                    lhs[0] if len(lhs) == 1 else jnp.concatenate(lhs, axis=0), w[k, tap], preferred_element_type=F32
                )
    for k, at in ((0, 0), (2, HEIGHT - 1)):
        raw[at] += shifted([products[k, tap][:WIDTH] for tap in range(3)], 1)[0]
    r = lax.broadcasted_iota(jnp.int32, (HEIGHT, DIM), 0)
    c = lax.broadcasted_iota(jnp.int32, (HEIGHT, 8, DIM), 1)
    for side, tap in ((0, 0), (1, 2)):
        y = [products[k, tap][-WIDTH:] for k in range(3)]
        above = jnp.where(r == 0, y[0][32:33], pltpu.roll(y[0][:HEIGHT], 1, 0))
        below = jnp.where(r == HEIGHT - 1, y[2][48:49], pltpu.roll(y[2][:HEIGHT], HEIGHT - 1, 0))
        more = (above + y[1][:HEIGHT] + below).reshape(HEIGHT, 1, DIM)
        if side == 0:
            raw[:, :8] += jnp.where(c == 0, more, 0.0)
        else:
            raw[:, WIDTH - 8 :] += jnp.where(c == 7, more, 0.0)

    for i in range(PATCHES // CHUNK):
        encoded = raw[i * ROWS : (i + 1) * ROWS].reshape(CHUNK, DIM).astype(BF16)
        wide = encoded.astype(F32)
        design[i * CHUNK : (i + 1) * CHUNK, :DIM] = encoded
        design[i * CHUNK : (i + 1) * CHUNK, DIM:] = (wide * wide).astype(BF16)

    for copy in to_partner + [offsets_partner]:
        copy.wait()

    def score(i, first, second):
        flipped = design[i * CHUNK : (i + 1) * CHUNK, :DIM].T
        wide = flipped.astype(F32)
        rhs = jnp.concatenate([flipped, (wide * wide).astype(BF16)], axis=0)
        lhs = jnp.concatenate([panel[first], panel[second]], axis=0)
        add = jnp.concatenate([offsets[first], offsets[second]], axis=0)
        scores = jnp.dot(lhs, rhs, preferred_element_type=F32) + jnp.concatenate([add] * (CHUNK // 128), axis=1)
        peak = jnp.max(scores, axis=0, keepdims=True)
        grown = jnp.exp(scores - peak)
        return peak, grown, jnp.sum(grown, axis=0, keepdims=True)

    def spread_offsets(block):
        for half in range(2):
            offsets[block, half * 128 : half * 128 + 128] = column(offset_lines[block, half, :1])

    spread_offsets(comp)
    spread_offsets(comp + 1 - 2 * core)
    near = []
    for i in range(PATCHES // CHUNK):
        peak, grown, total = score(i, comp, comp + 1 - 2 * core)
        mass[:, i * CHUNK : (i + 1) * CHUNK] = grown
        near.append((peak, total))

    offsets_across.wait()
    offsets_onward.start()
    for piece in range(PIECES):
        to_across[piece].wait()
        onward[piece].start()
    for copy in [offsets_onward] + onward:
        copy.wait()
    spread_offsets(far)
    spread_offsets(beyond)
    pl.semaphore_wait(heard.at[1], 3)
    limit = count[...]
    for i in range(PATCHES // CHUNK):
        at = slice(i * CHUNK, (i + 1) * CHUNK)
        peak, grown, total = score(i, far, beyond)
        near_peak, near_total = near[i]
        top = jnp.maximum(peak, near_peak)
        lift, near_lift = jnp.exp(peak - top), jnp.exp(near_peak - top)
        where = lax.broadcasted_iota(jnp.int32, (1, CHUNK), 1) + i * CHUNK
        scale = jnp.where(where < limit, 1.0 / (total * lift + near_total * near_lift), 0.0)
        for k, weight in ((0, mass[:, at] * (scale * near_lift)), (1, grown * (scale * lift))):
            rows = slice(k * 512, (k + 1) * 512)
            weight = weight.astype(BF16)
            gamma[rows, at] = weight
            weight = weight.astype(F32)
            part = weight[:, :128]
            for m in range(1, CHUNK // 128):
                part = part + weight[:, m * 128 : m * 128 + 128]
            if i == 0:
                zeroth[rows] = part
            else:
                zeroth[rows] += part

    tally = jnp.broadcast_to(limit.astype(F32), (1, 128))
    for h, order in ((0, 0), (1, 2)):
        for half in range(2):
            for ref, place in ((sums_held, order), (sums_give, order + 1)):
                start = place * BLOCK + half * 128
                ref[h, half, 0] = jnp.sum(zeroth[start : start + 128].T, axis=0, keepdims=True)
                ref[h, half, 1] = tally
    sums_copy = remote(sums_give, sums_take, sums_pair.at[0], sums_pair.at[1], partner)

    def statistics(place):
        stats = jnp.dot(gamma[place * BLOCK : (place + 1) * BLOCK, :], design[...], preferred_element_type=F32)
        return jnp.concatenate(
            [stats[:, :DIM].reshape(GROUP, 8, DIM), stats[:, DIM:].reshape(GROUP, 8, DIM)], axis=1
        )

    pair = []
    for k in range(2):
        pair.append(remote(give.at[k], take.at[k], pair_send.at[k], pair_recv.at[k], partner))
    for k in (1, 0):
        give[k] = statistics(2 * k + 1).astype(BF16)
        pair[k].start()
        if k == 1:
            sums_copy.start()

    sums_copy.wait()
    sums_held[...] += sums_take[...]

    def apart(number):
        return [number, number + 1 - 2 * lax.rem(number, 2), lax.rem(number + 2, 4), 3 - number]

    x_apart, z_apart = apart(row // 2), apart(col)
    y_apart = [lower, 1 - lower]

    def owners(k):
        hops = [0, 1, 2, 1]
        places = [(dx, dy, dz) for dx in range(4) for dy in range(2) for dz in range(4)]
        places = [p for p in places if k or any(p)]
        return sorted(places, key=lambda p: -(hops[p[0]] + hops[p[1] + 2 * k] + hops[p[2]]))

    def scatter(k):
        for dx, dy, dz in owners(k):
            to_row, to_col = 2 * x_apart[dx] + y_apart[dy], z_apart[dz]
            remote(
                held.at[k, to_row * 4 + to_col], landed.at[k * GROUP + dx * 8 + dy * 4 + dz],
                scatter_send, scatter_recv, (to_row, to_col, far if k else comp),
            ).start()

    owner = row * 4 + col
    adds = lax.rem(owner, 16) == 5
    lines_out = []
    for h, block in ((0, comp), (1, far)):
        for half in range(2):
            to = (4 * half + 1) * 8 + 2 + block // 2
            lines_out.append((to, remote(
                sums_held.at[h, half], sums_landed.at[lax.rem(me - to + CHIPS, CHIPS)],
                sums_send, sums_recv, (4 * half + 1, 1, block),
            )))
            @pl.when(to != me)
            def _():
                lines_out[-1][1].start()

    for k in (1, 0):
        mine = statistics(2 * k)
        pair[k].wait()
        held[k] = (mine + take[k].astype(F32)).astype(BF16)
        scatter(k)

    landed[0] = held[0, owner]

    def pass_on(step, carry):
        to = owner // 16 * 16 + lax.rem(lax.rem(owner, 16) + step, 16)
        remote(
            sums_total, sums_total, total_send, total_recv, (to // 4, lax.rem(to, 4), comp)
        ).start()
        return carry

    @pl.when(adds)
    def _():
        arrived = sums_landed.at[pl.ds(1, CHIPS - 1)]
        sums_landed[0] = sums_held[0, owner // 16]
        remote(arrived, arrived, sums_send, sums_recv, partner).wait_recv()
        sums_total[...] = jnp.sum(sums_landed[...], axis=0)
        lax.fori_loop(1, 16, pass_on, 0)

    for to, copy in lines_out:
        @pl.when(to != me)
        def _():
            copy.wait_send()

    rows = pl.ds(pl.multiple_of(owner * 8, 8), 8)
    centre = means[rows, :]
    inverse = precisions[rows, :]
    root = jnp.sqrt(inverse)
    share = jnp.exp(own_logs[rows, :1])
    all_but_own = landed.at[pl.ds(1, CHIPS - 1)]
    everyone = remote(all_but_own, all_but_own, scatter_send, scatter_recv, partner)
    everyone.wait_send()
    everyone.wait_recv()
    total = jnp.sum(landed[...].astype(F32), axis=0)

    @pl.when(adds)
    def _():
        sent = sums_landed.at[pl.ds(0, 15)]
        remote(sent, sent, total_send, total_recv, partner).wait_send()

    @pl.when(jnp.logical_not(adds))
    def _():
        remote(sums_total, sums_total, total_send, total_recv, partner).wait_recv()

    sums = sums_total[...]
    sums_column[...] = column(sums[0])
    patches = sums[1][:, :1]
    first = total[:8]
    second = total[8:]
    amount = sums_column[pl.ds(pl.multiple_of(lax.rem(owner, 16) * 8, 8), 8), :]
    amount = jnp.concatenate([amount, amount], axis=1)
    mean_fisher = (first - centre * amount) * root / jnp.sqrt(patches * share)
    var_fisher = (
        second * inverse - 2.0 * centre * inverse * first + (centre * centre * inverse - 1.0) * amount
    ) / jnp.sqrt(2.0 * patches * share)
    gathered[owner] = jnp.concatenate([mean_fisher, var_fisher], axis=0).astype(BF16)

    for dx, dy, dz in owners(0):
        remote(
            gathered.at[owner], gathered.at[owner], gather_send, gather_recv,
            (2 * x_apart[dx] + y_apart[dy], z_apart[dz], comp),
        ).start()
    others = remote(gathered.at[pl.ds(1, GROUP - 1)], gathered.at[pl.ds(1, GROUP - 1)], gather_send, gather_recv, partner)
    others.wait_send()
    others.wait_recv()
    out[...] = gathered[...]


def shards(features, conv_weight, conv_bias, means, precisions, mix_logits, tissue_counts):
    vmem = pl.BlockSpec(memory_space=pltpu.VMEM)
    hbm = pl.BlockSpec(memory_space=pltpu.HBM)
    dma = pltpu.SemaphoreType.DMA
    fisher = pl.pallas_call(
        kernel,
        out_shape=pltpu.VMEM((GROUP, 16, DIM), BF16),
        in_specs=[hbm] * 7,
        out_specs=vmem,
        scratch_shapes=[
            pltpu.VMEM((HEIGHT + 2, WIDTH, CHAN), BF16),
            pltpu.VMEM((3, 3, CHAN, DIM), BF16),
            pltpu.VMEM((1, DIM), F32),
            pltpu.VMEM((8, 1, 128), F32),
            pltpu.VMEM((1, 1), jnp.int32),
            pltpu.VMEM((BLOCK, DIM), F32),
            pltpu.VMEM((BLOCK, DIM), F32),
            pltpu.VMEM((2, WIDTH, CHAN), BF16),
            pltpu.VMEM((HEIGHT, WIDTH, DIM), F32),
            pltpu.VMEM((2, HEIGHT, CHAN), BF16),
            pltpu.VMEM((2, 2, 16, 128), BF16),
            pltpu.VMEM((2, 2, 16, 128), BF16),
            pltpu.VMEM((2, HEIGHT, CHAN), BF16),
            pltpu.VMEM((4, BLOCK, 2 * DIM), BF16),
            pltpu.VMEM((4, 2, 8, 128), F32),
            pltpu.VMEM((4, BLOCK, 128), F32),
            pltpu.VMEM((BLOCK, 128), F32),
            pltpu.VMEM((PATCHES, 2 * DIM), BF16),
            pltpu.VMEM((COMPS // 2, PATCHES), F32),
            pltpu.VMEM((COMPS, PATCHES), BF16),
            pltpu.VMEM((COMPS, 128), F32),
            pltpu.VMEM((2, GROUP, 16, DIM), BF16),
            pltpu.VMEM((2, GROUP, 16, DIM), BF16),
            pltpu.VMEM((2, GROUP, 16, DIM), BF16),
            pltpu.VMEM((CHIPS, 16, DIM), BF16),
            pltpu.VMEM((GROUP, 16, DIM), BF16),
            pltpu.VMEM((2, 2, 2, 1, 128), F32),
            pltpu.VMEM((2, 2, 2, 1, 128), F32),
            pltpu.VMEM((2, 2, 2, 1, 128), F32),
            pltpu.VMEM((CHIPS, 2, 1, 128), F32),
            pltpu.VMEM((2, 1, 128), F32),
            pltpu.VMEM((128, 128), F32),
            dma((7,)), dma((8,)), dma((8,)), dma((3, PIECES + 1)), dma((3, PIECES + 1)), dma((2,)), dma((2,)),
            dma((2,)), dma, dma, dma, dma, dma, dma, dma, dma, pltpu.SemaphoreType.REGULAR((2,)),
        ],
        compiler_params=pltpu.CompilerParams(
            collective_id=0, has_side_effects=True, vmem_limit_bytes=56 * 2**20
        ),
    )(
        features, conv_weight, conv_bias.reshape(1, DIM), means, precisions,
        mix_logits.reshape(8, 1, 128), tissue_counts,
    )
    return tuple(
        fisher[:, 8 * k : 8 * k + 8].astype(F32).reshape(BLOCK, DIM) for k in range(2)
    )


def solution(mesh):
    in_specs = (
        P("row", ("col", "comp"), None),
        P(),
        P(),
        P("comp", None),
        P("comp", None),
        P(),
        P("row", ("col", "comp")),
    )
    out_specs = (P("comp", None), P("comp", None))
    return jax.shard_map(shards, mesh=mesh, in_specs=in_specs, out_specs=out_specs, check_vma=False)
```
